256 devices in a mesh: grid: 16 (over z, core), tm: 16 (over y, x).
Axes of the slice: x: 4, y: 4, z: 8, core: 2. Of those that a mesh axis runs over, the one named last changes fastest.
Arguments:
- anomaly: bfloat16 [262144, 4096], P('grid', 'tm'), may hold values from -2000 to 2000
- start_basis: bfloat16 [32, 4096], P(None, 'tm'), may hold values from -6 to 6
Outputs:
- row_basis: float32 [32, 262144], P(None, 'grid')
- col_basis: float32 [32, 4096], P(None, 'tm')
The draws below stay inside these ranges and needn't reach their ends.
All inputs are finite; a program needn't handle non-finite values.
Results may differ from the reference program's by a relative error of at most 0.035.
Values may be sent and summed in bfloat16 or wider, within the bound.
No kernel may reach another device: no remote copies, remote signals or barrier semaphores. Data moves between devices by JAX's collectives and lax.ppermute only.
A program may use at most 64 MiB of HBM per device.

```python
import jax
import jax.numpy as jnp
from jax import lax

RANK = 32
ITERS = 6
G_DEV = 16384
T_DEV = 256
POINTS = 262144
HOURS = 4096
N_TM = 16


def draw_anomaly(key, part):
    key = jax.random.fold_in(key, 11)
    keys = jax.random.split(key, 7)
    regions = POINTS // G_DEV
    col_scale = jnp.exp(jax.random.uniform(keys[1], (1, HOURS), jnp.float32) * jnp.log(10.0))
    order = jnp.arange(RANK, dtype=jnp.float32) / (RANK - 1)
    strength = 3.0 * HOURS ** (-0.5) * jnp.power(0.4, order)
    weights = jnp.exp(jax.random.uniform(keys[5], (regions, RANK), jnp.float32) * jnp.log(10.0)) / jnp.sqrt(10.0)
    spatial = jnp.clip(jax.random.normal(keys[3], (POINTS, RANK), jnp.float32), -3.0, 3.0)
    spatial = spatial * jnp.repeat(weights, G_DEV, axis=0) * strength[None, :]
    temporal = jnp.clip(jax.random.normal(keys[4], (RANK, HOURS), jnp.float32), -3.0, 3.0)
    planted = jnp.dot(spatial, temporal, precision=lax.Precision.HIGHEST, preferred_element_type=jnp.float32)
    region_scale = jnp.exp(jax.random.uniform(keys[0], (regions, 1), jnp.float32) * jnp.log(10.0))
    jitter = jnp.exp(jax.random.uniform(keys[6], (POINTS, 1), jnp.float32) * jnp.log(3.0))
    noise = jnp.clip(jax.random.normal(keys[2], (POINTS, HOURS), jnp.float32), -6.0, 6.0)
    inner = jnp.clip(noise + planted, -6.0, 6.0)
    row_scale = jnp.repeat(region_scale, G_DEV, axis=0) * jitter
    return (inner * row_scale * col_scale).astype(jnp.bfloat16)


def shard_levels(stream_key, extent, pieces, low, high):
    def one(position, shards_of):
        draws = jax.random.uniform(jax.random.fold_in(jax.random.fold_in(stream_key, 6), position), (shards_of,), jnp.float32, low / len(pieces), high / len(pieces))
        return jnp.repeat(jnp.exp(draws), extent[position] // shards_of).reshape((-1,) + (1,) * (len(extent) - position - 1))

    level = one(*pieces[0])
    for cut in pieces[1:]:
        level = level * one(*cut)
    return level


def gaussian(stream_key, extent, scale, limit, shards=(), kind=jnp.bfloat16):
    factor_of = shard_levels(stream_key, extent, shards, -0.22, 0.18) if shards else 1.0
    entries = jax.random.normal(stream_key, extent, jnp.float32) * scale * factor_of
    return jnp.minimum(jnp.maximum(entries, -limit), limit).astype(kind)


def setup_inputs(seed: int = 0) -> dict:
    splits = jax.random.split(jax.random.key(seed), 3)
    return {
        "anomaly": draw_anomaly(jax.random.fold_in(splits[2], 71), 0),
        "start_basis": gaussian(splits[1], (RANK, HOURS), 1.0, 6.0, ((1, 16),)),
    }


def orthonormal(sketch, count):
    gram = jnp.dot(sketch.astype(jnp.float32), sketch.T.astype(jnp.float32), precision=lax.Precision.HIGHEST, preferred_element_type=jnp.float32) / count
    lower = jnp.linalg.cholesky(gram)
    return jax.scipy.linalg.solve_triangular(lower, sketch, lower=True)

def orthonormal_upper(block, count):
    return orthonormal(block[::-1], count)[::-1]

def reference(anomaly, start_basis):
    current = start_basis
    row_basis = None
    col_basis = None
    for step in range(ITERS):

        def add_block(index, total):
            columns = lax.dynamic_slice_in_dim(anomaly, index * T_DEV, T_DEV, 1)
            piece = lax.dynamic_slice_in_dim(current, index * T_DEV, T_DEV, 1)
            term = lax.dot_general(piece.astype(jnp.float32), columns.astype(jnp.float32), (((1,), (1,)), ((), ())), preferred_element_type=jnp.float32)
            return total + term.astype(jnp.bfloat16).astype(jnp.float32)
        sketch = lax.fori_loop(0, N_TM, add_block, jnp.zeros((RANK, POINTS), jnp.float32))
        row_basis = orthonormal(sketch, POINTS)
        row_cast = row_basis.astype(jnp.bfloat16)
        hours = jnp.dot(row_cast.astype(jnp.float32), anomaly.astype(jnp.float32), preferred_element_type=jnp.float32)
        col_basis = orthonormal_upper(hours, HOURS)
        current = col_basis.astype(jnp.bfloat16)
    return (row_basis, col_basis)
```

```python
import jax
import jax.numpy as jnp
from jax import lax
from jax.experimental import pallas as pl
from jax.experimental.pallas import tpu as pltpu
from jax.sharding import Mesh, PartitionSpec as P

ITERS = 6
RANK = 32
LANES = 128
EXTRA = RANK * RANK // LANES
ROWS = RANK + EXTRA
F32 = jnp.float32
BF16 = jnp.bfloat16
HIGH = lax.Precision.HIGHEST
NT = (((1,), (1,)), ((), ()))


def split_bf16(value):
    high = value.astype(BF16)
    low = (value - high.astype(F32)).astype(BF16)
    return jnp.concatenate([high, low], axis=0)


def packed_gram(block):
    tiled = jnp.concatenate([block] * (LANES // RANK), axis=0)
    wide = lax.dot_general(block, tiled, NT, precision=HIGH, preferred_element_type=F32)
    lane = lax.broadcasted_iota(jnp.int32, (EXTRA, LANES), 1) // RANK
    out = wide[0:EXTRA]
    for b in range(1, LANES // RANK):
        out = jnp.where(lane == b, wide[b * EXTRA : (b + 1) * EXTRA], out)
    return out


def inverse_factor(packed, upper):
    parts = RANK // EXTRA
    shape = (EXTRA, LANES)
    lane = lax.broadcasted_iota(jnp.int32, shape, 1)
    sub = lax.broadcasted_iota(jnp.int32, shape, 0)
    work = []
    for b in range(parts):
        shift = (RANK - b * RANK) % LANES
        gram = pltpu.roll(packed, shift, 1) if shift else packed
        gram = jnp.where(lane < 2 * RANK, gram, 0.0)
        work.append(jnp.where(lane < RANK, (lane == sub + b * EXTRA).astype(F32), gram))
    scale = []
    places = range(EXTRA - 1, -1, -1) if upper else range(EXTRA)
    for block in range(parts - 1, -1, -1) if upper else range(parts):
        beyond = range(block) if upper else range(block + 1, parts)
        cols = {
            b: [jnp.broadcast_to(work[b][:, c : c + 1], shape) for c in [RANK + block * EXTRA + r for r in places]]
            for b in (block, *beyond)
        }
        rows = [jnp.broadcast_to(work[block][r : r + 1, :], shape) for r in places]
        pivots = [[jnp.broadcast_to(col[r : r + 1, :], shape) for col in cols[block]] for r in places]
        scaled = []
        final = work[block]
        diagonal = pivots[0][0]
        for i, r in enumerate(places):
            inverse = 1.0 / pivots[i][i]
            for j in range(i + 1, EXTRA):
                factor = pivots[i][j] * inverse
                for k in range(j, EXTRA):
                    pivots[j][k] = pivots[j][k] - factor * pivots[i][k]
                rows[j] = rows[j] - factor * rows[i]
                for b in beyond:
                    cols[b][j] = cols[b][j] - factor * cols[b][i]
            scaled.append(rows[i] * inverse)
            final = jnp.where(sub == r, rows[i], final)
            diagonal = jnp.where(sub == r, pivots[i][i], diagonal)
        work[block] = final
        scale.append((block, diagonal))
        for b in beyond:
            for i in range(EXTRA):
                work[b] = work[b] - cols[b][i] * scaled[i]
    rows = [work[b] / jnp.sqrt(diagonal) for b, diagonal in sorted(scale, key=lambda item: item[0])]
    return jnp.concatenate(rows, axis=0)[:, :RANK]


def main_kernel(points, hours, first, keep, h_ref, a_ref, out_ref, s_ref, a_vmem, acc, sems):
    blocks, depth, width = a_vmem.shape
    for t in range(blocks):
        pltpu.make_async_copy(a_ref.at[t], a_vmem.at[t], sems.at[t]).start()
    if not first:
        total = h_ref[0, RANK:ROWS, :]
        for k in range(1, 2 * blocks):
            total = total + h_ref[k, RANK:ROWS, :]
        u_inv = inverse_factor(total, True) * float(hours) ** 0.5
    for t in range(blocks):
        if first:
            left = h_ref[t]
        else:
            left = split_bf16(jnp.concatenate([h_ref[t, 0:RANK, :], h_ref[blocks + t, 0:RANK, :]], axis=1))
        pltpu.make_async_copy(a_ref.at[t], a_vmem.at[t], sems.at[t]).wait()
        term = lax.dot_general(left, a_vmem[t], NT, preferred_element_type=F32)
        if t == 0:
            acc[0 : left.shape[0], :] = term
        else:
            acc[0 : left.shape[0], :] += term
    if first:
        sketch = acc[0:RANK, :]
    else:
        sketch = jnp.dot(
            u_inv, acc[0:RANK, :] + acc[RANK : 2 * RANK, :], precision=HIGH, preferred_element_type=F32
        )
    if keep:
        s_ref[...] = sketch.astype(BF16)
    gram = packed_gram(sketch)
    left = split_bf16(sketch)
    for t in range(blocks):
        both = jnp.dot(left, a_vmem[t], preferred_element_type=F32)
        part = both[0:RANK] + both[RANK : 2 * RANK]
        out_ref[t, 0:RANK, :] = part[:, 0:LANES]
        out_ref[blocks + t, 0:RANK, :] = part[:, LANES : 2 * LANES]
        out_ref[t, RANK:ROWS, :] = gram
        out_ref[blocks + t, RANK:ROWS, :] = gram


def main_step(points, hours, first, keep, h, a):
    blocks, depth, width = a.shape

    def kernel(h_ref, a_ref, out_ref, *rest):
        s_ref, rest = (rest[0], rest[1:]) if keep else (None, rest)
        main_kernel(points, hours, first, keep, h_ref, a_ref, out_ref, s_ref, *rest)

    out_shape = [jax.ShapeDtypeStruct((2 * blocks, ROWS, LANES), F32)]
    if keep:
        out_shape.append(jax.ShapeDtypeStruct((RANK, depth), BF16))
    return pl.pallas_call(
        kernel,
        out_shape=out_shape,
        in_specs=[pl.BlockSpec(memory_space=pltpu.VMEM), pl.BlockSpec(memory_space=pl.ANY)],
        out_specs=[pl.BlockSpec(memory_space=pltpu.VMEM)] * len(out_shape),
        scratch_shapes=[
            pltpu.VMEM(a.shape, BF16),
            pltpu.VMEM((2 * RANK, depth), F32),
            pltpu.SemaphoreType.DMA((blocks,)),
        ],
        compiler_params=pltpu.CompilerParams(vmem_limit_bytes=52 * 1024 * 1024),
        name="sketch_and_hours",
    )(h, a)


def sum_step(parts, copies):
    def kernel(in_ref, out_ref):
        total = in_ref[0]
        for k in range(1, parts.shape[0]):
            total = total + in_ref[k]
        for k in range(copies):
            out_ref[k] = total

    return pl.pallas_call(
        kernel,
        out_shape=jax.ShapeDtypeStruct((copies,) + parts.shape[1:], F32),
        in_specs=[pl.BlockSpec(memory_space=pltpu.VMEM)],
        out_specs=pl.BlockSpec(memory_space=pltpu.VMEM),
        name="sum_parts",
    )(parts)


def hour_step(parts, copies, points):
    def kernel(in_ref, out_ref, l_ref):
        total = in_ref[0]
        for k in range(1, parts.shape[0]):
            total = total + in_ref[k]
        l_inv = inverse_factor(total[RANK:ROWS], False) * float(points) ** 0.5
        hours = jnp.dot(l_inv, total[0:RANK], precision=HIGH, preferred_element_type=F32)
        gram = packed_gram(hours)
        for k in range(copies):
            out_ref[k, 0:RANK, :] = hours
            out_ref[k, RANK:ROWS, :] = gram
        l_ref[...] = l_inv

    return pl.pallas_call(
        kernel,
        out_shape=[
            jax.ShapeDtypeStruct((copies, ROWS, LANES), F32),
            jax.ShapeDtypeStruct((RANK, RANK), F32),
        ],
        in_specs=[pl.BlockSpec(memory_space=pltpu.VMEM)],
        out_specs=[pl.BlockSpec(memory_space=pltpu.VMEM)] * 2,
        name="row_factor",
    )(parts)


def column_step(h, mine, hours):
    def kernel(h_ref, mine_ref, out_ref):
        total = h_ref[0, RANK:ROWS, :]
        for k in range(1, h_ref.shape[0]):
            total = total + h_ref[k, RANK:ROWS, :]
        u_inv = inverse_factor(total, True) * float(hours) ** 0.5
        block = jnp.concatenate([mine_ref[0, 0:RANK, :], mine_ref[1, 0:RANK, :]], axis=1)
        out_ref[...] = jnp.dot(u_inv, block, precision=HIGH, preferred_element_type=F32)

    return pl.pallas_call(
        kernel,
        out_shape=jax.ShapeDtypeStruct((RANK, 2 * LANES), F32),
        in_specs=[pl.BlockSpec(memory_space=pltpu.VMEM)] * 2,
        out_specs=pl.BlockSpec(memory_space=pltpu.VMEM),
        name="column_factor",
    )(h, mine)


def row_step(l_inv, sketch):
    def kernel(l_ref, s_ref, out_ref):
        value = l_ref[...]
        pieces = []
        for _ in range(3):
            piece = value.astype(BF16)
            pieces.append(piece)
            value = value - piece.astype(F32)
        left = jnp.concatenate(pieces, axis=0)
        out = jnp.dot(left, s_ref[0], preferred_element_type=F32)
        out_ref[...] = out[0:RANK] + out[RANK : 2 * RANK] + out[2 * RANK : 3 * RANK]

    blocks, _, depth = sketch.shape
    return pl.pallas_call(
        kernel,
        grid=(blocks,),
        out_shape=jax.ShapeDtypeStruct((RANK, blocks * depth), F32),
        in_specs=[
            pl.BlockSpec((RANK, RANK), lambda i: (0, 0)),
            pl.BlockSpec((1, RANK, depth), lambda i: (i, 0, 0)),
        ],
        out_specs=pl.BlockSpec((RANK, depth), lambda i: (0, i)),
        cost_estimate=pl.CostEstimate(
            flops=6 * RANK * RANK * blocks * depth, bytes_accessed=6 * RANK * blocks * depth, transcendentals=0
        ),
        name="row_basis",
    )(l_inv, sketch)


def solution(mesh):
    grid_size, tm_size = mesh.devices.shape
    fine = Mesh(mesh.devices.reshape(grid_size // 2, 2, tm_size), ("z", "c", "t"))

    def shards(anomaly, start_basis):
        points = anomaly.shape[0] * grid_size
        hours = anomaly.shape[1] * tm_size
        depth = anomaly.shape[0] // tm_size
        basis = jnp.broadcast_to(start_basis[None], (tm_size,) + start_basis.shape)
        h = lax.all_to_all(basis, "t", 0, 0)
        a = lax.all_to_all(anomaly.reshape(tm_size, depth, anomaly.shape[1]), "t", 0, 0)
        for step in range(ITERS):
            last = step == ITERS - 1
            out = main_step(points, hours, step == 0, last, h, a)
            if last:
                rows = lax.all_gather(out[1], "t", axis=0)
            part = lax.all_to_all(out[0], ("c", "t"), 0, 0)
            part = sum_step(part, grid_size // 2)
            part = lax.all_to_all(part, "z", 0, 0)
            h, l_inv = hour_step(part, 2 * tm_size, points)
            h = lax.all_to_all(h, ("c", "t"), 0, 0)
        place = lax.axis_index("t")
        mine = lax.dynamic_index_in_dim(h.reshape(2, tm_size, ROWS, LANES), place, 1, False)
        return row_step(l_inv, rows), column_step(h, mine, hours)

    return jax.shard_map(
        shards,
        mesh=fine,
        in_specs=(P(("z", "c"), "t"), P(None, "t")),
        out_specs=(P(None, ("z", "c")), P(None, "t")),
        check_vma=False,
    )
```

```python
import jax
import jax.numpy as jnp
from jax import lax
from jax.experimental import pallas as pl
from jax.experimental.pallas import tpu as pltpu
from jax.sharding import Mesh, PartitionSpec as P

ITERS = 6
RANK = 32
LANES = 128
EXTRA = RANK * RANK // LANES
ROWS = RANK + EXTRA
F32 = jnp.float32
BF16 = jnp.bfloat16
HIGH = lax.Precision.HIGHEST
NT = (((1,), (1,)), ((), ()))
TN = (((0,), (0,)), ((), ()))


def split_bf16(value):
    high = value.astype(BF16)
    low = (value - high.astype(F32)).astype(BF16)
    return jnp.concatenate([high, low], axis=0)


def pack(wide):
    lane = lax.broadcasted_iota(jnp.int32, (EXTRA, LANES), 1) // RANK
    out = wide[0:EXTRA]
    for b in range(1, LANES // RANK):
        out = jnp.where(lane == b, wide[b * EXTRA : (b + 1) * EXTRA], out)
    return out


def packed_gram(block):
    tiled = jnp.concatenate([block] * (LANES // RANK), axis=0)
    return pack(lax.dot_general(block, tiled, NT, precision=HIGH, preferred_element_type=F32))


def inverse_factor(packed, upper):
    parts = RANK // EXTRA
    shape = (EXTRA, LANES)
    lane = lax.broadcasted_iota(jnp.int32, shape, 1)
    sub = lax.broadcasted_iota(jnp.int32, shape, 0)
    work = []
    for b in range(parts):
        shift = (RANK - b * RANK) % LANES
        gram = pltpu.roll(packed, shift, 1) if shift else packed
        gram = jnp.where(lane < 2 * RANK, gram, 0.0)
        work.append(jnp.where(lane < RANK, (lane == sub + b * EXTRA).astype(F32), gram))
    scale = []
    places = range(EXTRA - 1, -1, -1) if upper else range(EXTRA)
    for block in range(parts - 1, -1, -1) if upper else range(parts):
        beyond = range(block) if upper else range(block + 1, parts)
        cols = {
            b: [jnp.broadcast_to(work[b][:, c : c + 1], shape) for c in [RANK + block * EXTRA + r for r in places]]
            for b in (block, *beyond)
        }
        rows = [jnp.broadcast_to(work[block][r : r + 1, :], shape) for r in places]
        pivots = [[jnp.broadcast_to(col[r : r + 1, :], shape) for col in cols[block]] for r in places]
        scaled = []
        final = work[block]
        diagonal = pivots[0][0]
        for i, r in enumerate(places):
            inverse = 1.0 / pivots[i][i]
            for j in range(i + 1, EXTRA):
                factor = pivots[i][j] * inverse
                for k in range(j, EXTRA):
                    pivots[j][k] = pivots[j][k] - factor * pivots[i][k]
                rows[j] = rows[j] - factor * rows[i]
                for b in beyond:
                    cols[b][j] = cols[b][j] - factor * cols[b][i]
            scaled.append(rows[i] * inverse)
            final = jnp.where(sub == r, rows[i], final)
            diagonal = jnp.where(sub == r, pivots[i][i], diagonal)
        work[block] = final
        scale.append((block, diagonal))
        for b in beyond:
            for i in range(EXTRA):
                work[b] = work[b] - cols[b][i] * scaled[i]
    rows = [work[b] / jnp.sqrt(diagonal) for b, diagonal in sorted(scale, key=lambda item: item[0])]
    return jnp.concatenate(rows, axis=0)[:, :RANK]


def append_basis(a, basis):
    blocks, depth, width = a.shape

    def kernel(a_ref, basis_ref, out_ref, held, in_sems, out_sems):
        def load(t):
            return pltpu.make_async_copy(a_ref.at[t], held.at[t, 0:depth, :], in_sems.at[t])

        def store(t):
            return pltpu.make_async_copy(held.at[t], out_ref.at[t], out_sems.at[t])

        for t in range(blocks):
            load(t).start()
        for t in range(blocks):
            held[t, depth : depth + RANK, :] = basis_ref[...]
            load(t).wait()
            store(t).start()
        for t in range(blocks):
            store(t).wait()

    return pl.pallas_call(
        kernel,
        out_shape=jax.ShapeDtypeStruct((blocks, depth + RANK, width), BF16),
        in_specs=[pl.BlockSpec(memory_space=pl.ANY), pl.BlockSpec(memory_space=pltpu.VMEM)],
        out_specs=pl.BlockSpec(memory_space=pl.ANY),
        scratch_shapes=[
            pltpu.VMEM((blocks, depth + RANK, width), BF16),
            pltpu.SemaphoreType.DMA((blocks,)),
            pltpu.SemaphoreType.DMA((blocks,)),
        ],
        compiler_params=pltpu.CompilerParams(vmem_limit_bytes=52 * 1024 * 1024),
        name="append_basis",
    )(a, basis)


def main_step(hours, first, keep, h, a):
    blocks, depth, width = a.shape
    depth -= RANK

    def kernel(*refs):
        h_ref, a_ref, out_ref, *refs = ([None] if first else []) + list(refs)
        s_ref = refs[0] if keep else None
        a_vmem, acc, sems = refs[-3:]
        length = a_vmem.shape[1]

        def copy(t):
            return pltpu.make_async_copy(a_ref.at[t, 0:length, :], a_vmem.at[t], sems.at[t])

        for t in range(blocks):
            copy(t).start()
        if not first:
            parts = [jnp.concatenate([h_ref[t], h_ref[blocks + t]], axis=1) for t in range(blocks)]
        for t in range(blocks):
            copy(t).wait()
            part = a_vmem[t, depth : depth + RANK, :] if first else parts[t]
            term = lax.dot_general(part, a_vmem[t, 0:depth, :], NT, preferred_element_type=F32)
            if t == 0:
                acc[...] = term
            else:
                acc[...] += term
        sketch = acc[...]
        if not first:
            whole = jnp.concatenate(parts, axis=1)
            tiled = jnp.concatenate([whole] * (LANES // RANK), axis=0)
            gram = pack(lax.dot_general(whole, tiled, NT, preferred_element_type=F32))
            v_inv = inverse_factor(gram, True) * float(hours) ** 0.5
            sketch = jnp.dot(v_inv, sketch, precision=HIGH, preferred_element_type=F32)
        if keep:
            s_ref[...] = sketch.astype(BF16)
        gram = packed_gram(sketch)
        left = split_bf16(sketch)
        for t in range(blocks):
            both = jnp.dot(left, a_vmem[t, 0:depth, :], preferred_element_type=F32)
            part = both[0:RANK] + both[RANK : 2 * RANK]
            out_ref[t, 0:RANK, :] = part[:, 0:LANES]
            out_ref[blocks + t, 0:RANK, :] = part[:, LANES : 2 * LANES]
            out_ref[t, RANK:ROWS, :] = gram
            out_ref[blocks + t, RANK:ROWS, :] = gram

    operands = (a,) if first else (h, a)
    out_shape = [jax.ShapeDtypeStruct((2 * blocks, ROWS, LANES), F32)]
    if keep:
        out_shape.append(jax.ShapeDtypeStruct((RANK, depth), BF16))
    return pl.pallas_call(
        kernel,
        out_shape=out_shape,
        in_specs=[pl.BlockSpec(memory_space=pltpu.VMEM)] * len(operands[1:]) + [pl.BlockSpec(memory_space=pl.ANY)],
        out_specs=[pl.BlockSpec(memory_space=pltpu.VMEM)] * len(out_shape),
        scratch_shapes=[
            pltpu.VMEM((blocks, depth + (RANK if first else 0), width), BF16),
            pltpu.VMEM((RANK, depth), F32),
            pltpu.SemaphoreType.DMA((blocks,)),
        ],
        compiler_params=pltpu.CompilerParams(vmem_limit_bytes=52 * 1024 * 1024),
        name="sketch_and_hours",
    )(*operands)


def sum_step(parts, copies):
    def kernel(in_ref, out_ref):
        total = in_ref[0]
        for k in range(1, parts.shape[0]):
            total = total + in_ref[k]
        for k in range(copies):
            out_ref[k] = total

    return pl.pallas_call(
        kernel,
        out_shape=jax.ShapeDtypeStruct((copies,) + parts.shape[1:], F32),
        in_specs=[pl.BlockSpec(memory_space=pltpu.VMEM)],
        out_specs=pl.BlockSpec(memory_space=pltpu.VMEM),
        name="sum_parts",
    )(parts)


def hour_step(parts, copies, points, last):
    def kernel(in_ref, *outs):
        total = in_ref[0]
        for k in range(1, parts.shape[0]):
            total = total + in_ref[k]
        l_inv = inverse_factor(total[RANK:ROWS], False) * float(points) ** 0.5
        hours = jnp.dot(l_inv, total[0:RANK], precision=HIGH, preferred_element_type=F32)
        hours = lax.dot_general(l_inv, hours, TN, precision=HIGH, preferred_element_type=F32)
        if last:
            gram = packed_gram(hours)
            for k in range(copies):
                outs[0][k] = gram
            outs[1][...] = hours
            outs[2][...] = l_inv
        else:
            rounded = hours.astype(BF16)
            for k in range(copies):
                outs[0][k] = rounded

    out_shape = [jax.ShapeDtypeStruct((copies, RANK, LANES), BF16)]
    if last:
        out_shape = [
            jax.ShapeDtypeStruct((copies, EXTRA, LANES), F32),
            jax.ShapeDtypeStruct((RANK, LANES), F32),
            jax.ShapeDtypeStruct((RANK, RANK), F32),
        ]
    return pl.pallas_call(
        kernel,
        out_shape=out_shape,
        in_specs=[pl.BlockSpec(memory_space=pltpu.VMEM)],
        out_specs=[pl.BlockSpec(memory_space=pltpu.VMEM)] * len(out_shape),
        name="row_factor",
    )(parts)


def column_step(grams, mine, other, core, hours):
    def kernel(core_ref, gram_ref, mine_ref, other_ref, out_ref):
        total = gram_ref[0]
        for k in range(1, grams.shape[0]):
            total = total + gram_ref[k]
        v_inv = inverse_factor(total, True) * float(hours) ** 0.5
        first = core_ref[0] == 0
        low = jnp.where(first, mine_ref[...], other_ref[...])
        high = jnp.where(first, other_ref[...], mine_ref[...])
        block = jnp.concatenate([low, high], axis=1)
        out_ref[...] = jnp.dot(v_inv, block, precision=HIGH, preferred_element_type=F32)

    return pl.pallas_call(
        kernel,
        out_shape=jax.ShapeDtypeStruct((RANK, 2 * LANES), F32),
        in_specs=[pl.BlockSpec(memory_space=pltpu.SMEM)] + [pl.BlockSpec(memory_space=pltpu.VMEM)] * 3,
        out_specs=pl.BlockSpec(memory_space=pltpu.VMEM),
        name="column_factor",
    )(core, grams, mine, other)


def row_step(l_inv, sketch):
    blocks, _, depth = sketch.shape
    group = 4

    def kernel(l_ref, s_ref, out_ref):
        value = l_ref[...]
        pieces = []
        for _ in range(3):
            piece = value.astype(BF16)
            pieces.append(piece)
            value = value - piece.astype(F32)
        left = jnp.concatenate(pieces, axis=0)
        for k in range(group):
            out = jnp.dot(left, s_ref[k], preferred_element_type=F32)
            out = out[0:RANK] + out[RANK : 2 * RANK] + out[2 * RANK : 3 * RANK]
            out_ref[:, k * depth : (k + 1) * depth] = out

    return pl.pallas_call(
        kernel,
        grid=(blocks // group,),
        out_shape=jax.ShapeDtypeStruct((RANK, blocks * depth), F32),
        in_specs=[
            pl.BlockSpec((RANK, RANK), lambda i: (0, 0)),
            pl.BlockSpec((group, RANK, depth), lambda i: (i, 0, 0)),
        ],
        out_specs=pl.BlockSpec((RANK, group * depth), lambda i: (0, i)),
        cost_estimate=pl.CostEstimate(
            flops=6 * RANK * RANK * blocks * depth, bytes_accessed=6 * RANK * blocks * depth, transcendentals=0
        ),
        name="row_basis",
    )(l_inv, sketch)


def ring(size, shift):
    return [(i, (i + shift) % size) for i in range(size)]


def solution(mesh):
    grid_size, tm_size = mesh.devices.shape
    fine = Mesh(mesh.devices.reshape(grid_size // 2, 2, tm_size), ("z", "c", "t"))

    def shards(anomaly, start_basis):
        points = anomaly.shape[0] * grid_size
        hours = anomaly.shape[1] * tm_size
        depth = anomaly.shape[0] // tm_size
        core = lax.axis_index("c").reshape(1).astype(jnp.int32)
        a = append_basis(anomaly.reshape(tm_size, depth, anomaly.shape[1]), start_basis)
        a = lax.all_to_all(a, "t", 0, 0)
        for step in range(ITERS):
            last = step == ITERS - 1
            out = main_step(hours, step == 0, last, a if step == 0 else h, a)
            if last:
                rows = lax.all_gather(out[1], "t", axis=0)
            part = lax.all_to_all(out[0], ("c", "t"), 0, 0)
            part = sum_step(part, grid_size // 2)
            part = lax.all_to_all(part, "z", 0, 0)
            out = hour_step(part, 2 * tm_size, points, last)
            h = lax.all_to_all(out[0], ("c", "t"), 0, 0)
        mine = out[1]
        other = lax.ppermute(mine, "c", ring(2, 1))
        return row_step(out[2], rows), column_step(h, mine, other, core, hours)

    return jax.shard_map(
        shards,
        mesh=fine,
        in_specs=(P(("z", "c"), "t"), P(None, "t")),
        out_specs=(P(None, ("z", "c")), P(None, "t")),
        check_vma=False,
    )
```

```python
import jax
import jax.numpy as jnp
from jax import lax
from jax.experimental import pallas as pl
from jax.experimental.pallas import tpu as pltpu
from jax.sharding import Mesh, PartitionSpec as P

ITERS = 6
RANK = 32
LANES = 128
EXTRA = RANK * RANK // LANES
ROWS = RANK + EXTRA
SMALL_BYTES = 4 * 1024 * 1024
MID_BYTES = 20 * 1024 * 1024
F32 = jnp.float32
BF16 = jnp.bfloat16
HIGH = lax.Precision.HIGHEST
NT = (((1,), (1,)), ((), ()))
TN = (((0,), (0,)), ((), ()))


def split_bf16(value):
    high = value.astype(BF16)
    low = (value - high.astype(F32)).astype(BF16)
    return jnp.concatenate([high, low], axis=0)


def pack(wide):
    lane = lax.broadcasted_iota(jnp.int32, (EXTRA, LANES), 1) // RANK
    out = wide[0:EXTRA]
    for b in range(1, LANES // RANK):
        out = jnp.where(lane == b, wide[b * EXTRA : (b + 1) * EXTRA], out)
    return out


def packed_gram(block):
    tiled = jnp.concatenate([block] * (LANES // RANK), axis=0)
    return pack(lax.dot_general(block, tiled, NT, precision=HIGH, preferred_element_type=F32))


def inverse_factor(packed, upper):
    parts = RANK // EXTRA
    shape = (EXTRA, LANES)
    lane = lax.broadcasted_iota(jnp.int32, shape, 1)
    sub = lax.broadcasted_iota(jnp.int32, shape, 0)
    work = []
    for b in range(parts):
        shift = (RANK - b * RANK) % LANES
        gram = pltpu.roll(packed, shift, 1) if shift else packed
        gram = jnp.where(lane < 2 * RANK, gram, 0.0)
        work.append(jnp.where(lane < RANK, (lane == sub + b * EXTRA).astype(F32), gram))
    scale = []
    places = range(EXTRA - 1, -1, -1) if upper else range(EXTRA)
    for block in range(parts - 1, -1, -1) if upper else range(parts):
        beyond = range(block) if upper else range(block + 1, parts)
        cols = {
            b: [jnp.broadcast_to(work[b][:, c : c + 1], shape) for c in [RANK + block * EXTRA + r for r in places]]
            for b in (block, *beyond)
        }
        rows = [jnp.broadcast_to(work[block][r : r + 1, :], shape) for r in places]
        pivots = [[jnp.broadcast_to(col[r : r + 1, :], shape) for col in cols[block]] for r in places]
        scaled = []
        final = work[block]
        diagonal = pivots[0][0]
        for i, r in enumerate(places):
            inverse = 1.0 / pivots[i][i]
            for j in range(i + 1, EXTRA):
                factor = pivots[i][j] * inverse
                for k in range(j, EXTRA):
                    pivots[j][k] = pivots[j][k] - factor * pivots[i][k]
                rows[j] = rows[j] - factor * rows[i]
                for b in beyond:
                    cols[b][j] = cols[b][j] - factor * cols[b][i]
            scaled.append(rows[i] * inverse)
            final = jnp.where(sub == r, rows[i], final)
            diagonal = jnp.where(sub == r, pivots[i][i], diagonal)
        work[block] = final
        scale.append((block, diagonal))
        for b in beyond:
            for i in range(EXTRA):
                work[b] = work[b] - cols[b][i] * scaled[i]
    rows = [work[b] / jnp.sqrt(diagonal) for b, diagonal in sorted(scale, key=lambda item: item[0])]
    return jnp.concatenate(rows, axis=0)[:, :RANK]


def append_basis(a, basis):
    blocks, depth, width = a.shape

    def kernel(a_ref, basis_ref, out_ref, sems):
        def load(t):
            return pltpu.make_async_copy(a_ref.at[t], out_ref.at[t, 0:depth, :], sems.at[t])

        for t in range(blocks):
            load(t).start()
        for t in range(blocks):
            out_ref[t, depth : depth + RANK, :] = basis_ref[...]
        for t in range(blocks):
            load(t).wait()

    return pl.pallas_call(
        kernel,
        out_shape=jax.ShapeDtypeStruct((blocks, depth + RANK, width), BF16),
        in_specs=[pl.BlockSpec(memory_space=pl.ANY), pl.BlockSpec(memory_space=pltpu.VMEM)],
        out_specs=pl.BlockSpec(memory_space=pltpu.VMEM),
        scratch_shapes=[pltpu.SemaphoreType.DMA((blocks,))],
        compiler_params=pltpu.CompilerParams(vmem_limit_bytes=MID_BYTES),
        name="append_basis",
    )(a, basis)


def first_step(core, a):
    blocks, depth, width = a.shape
    depth -= RANK
    half = blocks // 2

    def kernel(core_ref, a_ref, out_ref, send_ref, acc, send_sems):
        def send(i):
            t = (1 - core_ref[0]) * half + i
            return pltpu.make_async_copy(a_ref.at[t, 0:depth, :], send_ref.at[i], send_sems.at[i])

        for i in range(half):
            send(i).start()
        for t in range(blocks):
            basis = a_ref[t, depth : depth + RANK, :]
            term = lax.dot_general(basis, a_ref[t, 0:depth, :], NT, preferred_element_type=F32)
            if t == 0:
                acc[...] = term
            else:
                acc[...] += term
        sketch = acc[...]
        gram = packed_gram(sketch)
        left = split_bf16(sketch)
        for t in range(blocks):
            both = jnp.dot(left, a_ref[t, 0:depth, :], preferred_element_type=F32)
            store_part(out_ref, t, both[0:RANK] + both[RANK : 2 * RANK], gram)
        for i in range(half):
            send(i).wait()

    return pl.pallas_call(
        kernel,
        out_shape=[
            jax.ShapeDtypeStruct((2 * blocks, ROWS, LANES), F32),
            jax.ShapeDtypeStruct((half, depth, width), BF16),
        ],
        in_specs=[pl.BlockSpec(memory_space=pltpu.SMEM), pl.BlockSpec(memory_space=pltpu.VMEM)],
        out_specs=[pl.BlockSpec(memory_space=pltpu.VMEM), pl.BlockSpec(memory_space=pl.ANY)],
        scratch_shapes=[pltpu.VMEM((RANK, depth), F32), pltpu.SemaphoreType.DMA((half,))],
        compiler_params=pltpu.CompilerParams(vmem_limit_bytes=MID_BYTES),
        name="first_products",
    )(core, a)


def store_part(out_ref, block, part, gram):
    for side in range(2):
        out_ref[2 * block + side, 0:RANK, :] = part[:, side * LANES : (side + 1) * LANES]
        out_ref[2 * block + side, RANK:ROWS, :] = gram


def sketch_step(core, h, a, mate):
    half, depth, width = mate.shape

    def kernel(core_ref, h_ref, a_ref, mate_ref, out_ref):
        parts = [jnp.concatenate([h_ref[2 * i], h_ref[2 * i + 1]], axis=1) for i in range(half)]
        for side in range(2):
            rows = slice(side * RANK, (side + 1) * RANK)
            for i in range(half):
                block = mate_ref[i] if side else a_ref[core_ref[0] * half + i, 0:depth, :]
                term = lax.dot_general(parts[i], block, NT, preferred_element_type=F32)
                if i == 0:
                    out_ref[rows, :] = term
                else:
                    out_ref[rows, :] += term
        whole = jnp.concatenate(parts, axis=1)
        tiled = jnp.concatenate([whole] * (LANES // RANK), axis=0)
        out_ref[2 * RANK :, :] = jnp.zeros((EXTRA, depth), F32)
        out_ref[2 * RANK :, 0:LANES] = pack(lax.dot_general(whole, tiled, NT, preferred_element_type=F32))

    return pl.pallas_call(
        kernel,
        out_shape=jax.ShapeDtypeStruct((2 * RANK + EXTRA, depth), F32),
        in_specs=[
            pl.BlockSpec(memory_space=pltpu.SMEM),
            pl.BlockSpec(memory_space=pltpu.VMEM),
            pl.BlockSpec(memory_space=pltpu.VMEM),
            pl.BlockSpec(memory_space=pltpu.VMEM),
        ],
        out_specs=pl.BlockSpec(memory_space=pltpu.VMEM),
        compiler_params=pltpu.CompilerParams(vmem_limit_bytes=MID_BYTES),
        name="partial_sketch",
    )(core, h, a, mate)


def product_step(hours, keep, core, mine, other, a, mate):
    half, depth, width = mate.shape

    def kernel(core_ref, mine_ref, other_ref, a_ref, mate_ref, out_ref, *refs):
        gram = mine_ref[2 * RANK :, 0:LANES] + other_ref[2 * RANK :, 0:LANES]
        v_inv = inverse_factor(gram, True) * float(hours) ** 0.5
        own = mine_ref[0:RANK, :] + other_ref[RANK : 2 * RANK, :]
        own = jnp.dot(v_inv, own, precision=HIGH, preferred_element_type=F32)
        if keep:
            refs[0][...] = own.astype(BF16)
        far = mine_ref[RANK : 2 * RANK, :] + other_ref[0:RANK, :]
        far = jnp.dot(v_inv, far, precision=HIGH, preferred_element_type=F32)
        gram = packed_gram(own) + packed_gram(far)
        left = split_bf16(own)
        right = split_bf16(far)
        for i in range(half):
            both = jnp.dot(left, a_ref[core_ref[0] * half + i, 0:depth, :], preferred_element_type=F32)
            both = both + jnp.dot(right, mate_ref[i], preferred_element_type=F32)
            store_part(out_ref, i, both[0:RANK] + both[RANK : 2 * RANK], gram)

    out_shape = [jax.ShapeDtypeStruct((2 * half, ROWS, LANES), F32)]
    if keep:
        out_shape.append(jax.ShapeDtypeStruct((RANK, depth), BF16))
    return pl.pallas_call(
        kernel,
        out_shape=out_shape,
        in_specs=[
            pl.BlockSpec(memory_space=pltpu.SMEM),
            pl.BlockSpec(memory_space=pltpu.VMEM),
            pl.BlockSpec(memory_space=pltpu.VMEM),
            pl.BlockSpec(memory_space=pltpu.VMEM),
            pl.BlockSpec(memory_space=pltpu.VMEM),
        ],
        out_specs=[pl.BlockSpec(memory_space=pltpu.VMEM)] * len(out_shape),
        compiler_params=pltpu.CompilerParams(vmem_limit_bytes=MID_BYTES),
        name="hour_products",
    )(core, mine, other, a, mate)


def sum_step(parts, copies):
    def kernel(in_ref, out_ref):
        total = in_ref[0]
        for k in range(1, parts.shape[0]):
            total = total + in_ref[k]
        for k in range(copies):
            out_ref[k] = total

    return pl.pallas_call(
        kernel,
        out_shape=jax.ShapeDtypeStruct((copies,) + parts.shape[1:], F32),
        in_specs=[pl.BlockSpec(memory_space=pltpu.VMEM)],
        out_specs=pl.BlockSpec(memory_space=pltpu.VMEM),
        compiler_params=pltpu.CompilerParams(vmem_limit_bytes=SMALL_BYTES),
        name="sum_parts",
    )(parts)


def hour_step(parts, copies, points, last):
    def kernel(in_ref, *outs):
        total = in_ref[0]
        for k in range(1, parts.shape[0]):
            total = total + in_ref[k]
        l_inv = inverse_factor(total[RANK:ROWS], False) * float(points) ** 0.5
        hours = jnp.dot(l_inv, total[0:RANK], precision=HIGH, preferred_element_type=F32)
        hours = lax.dot_general(l_inv, hours, TN, precision=HIGH, preferred_element_type=F32)
        if last:
            gram = packed_gram(hours)
            for k in range(copies):
                outs[0][k] = gram
            outs[1][...] = hours
            outs[2][...] = l_inv
        else:
            rounded = hours.astype(BF16)
            for k in range(copies):
                outs[0][k] = rounded

    out_shape = [jax.ShapeDtypeStruct((copies, RANK, LANES), BF16)]
    if last:
        out_shape = [
            jax.ShapeDtypeStruct((copies, EXTRA, LANES), F32),
            jax.ShapeDtypeStruct((RANK, LANES), F32),
            jax.ShapeDtypeStruct((RANK, RANK), F32),
        ]
    return pl.pallas_call(
        kernel,
        out_shape=out_shape,
        in_specs=[pl.BlockSpec(memory_space=pltpu.VMEM)],
        out_specs=[pl.BlockSpec(memory_space=pltpu.VMEM)] * len(out_shape),
        compiler_params=pltpu.CompilerParams(vmem_limit_bytes=SMALL_BYTES),
        name="row_factor",
    )(parts)


def column_step(grams, mine, other, core, hours):
    def kernel(core_ref, gram_ref, mine_ref, other_ref, out_ref):
        total = gram_ref[0]
        for k in range(1, grams.shape[0]):
            total = total + gram_ref[k]
        v_inv = inverse_factor(total, True) * float(hours) ** 0.5
        first = core_ref[0] == 0
        low = jnp.where(first, mine_ref[...], other_ref[...])
        high = jnp.where(first, other_ref[...], mine_ref[...])
        block = jnp.concatenate([low, high], axis=1)
        out_ref[...] = jnp.dot(v_inv, block, precision=HIGH, preferred_element_type=F32)

    return pl.pallas_call(
        kernel,
        out_shape=jax.ShapeDtypeStruct((RANK, 2 * LANES), F32),
        in_specs=[pl.BlockSpec(memory_space=pltpu.SMEM)] + [pl.BlockSpec(memory_space=pltpu.VMEM)] * 3,
        out_specs=pl.BlockSpec(memory_space=pltpu.VMEM),
        compiler_params=pltpu.CompilerParams(vmem_limit_bytes=SMALL_BYTES),
        name="column_factor",
    )(core, grams, mine, other)


def row_step(l_inv, sketch):
    blocks, _, depth = sketch.shape
    group = 4

    def kernel(l_ref, s_ref, out_ref):
        left = split_bf16(l_ref[...])
        for k in range(group):
            out = jnp.dot(left, s_ref[k], preferred_element_type=F32)
            out_ref[:, k * depth : (k + 1) * depth] = out[0:RANK] + out[RANK : 2 * RANK]

    return pl.pallas_call(
        kernel,
        grid=(blocks // group,),
        out_shape=jax.ShapeDtypeStruct((RANK, blocks * depth), F32),
        in_specs=[
            pl.BlockSpec((RANK, RANK), lambda i: (0, 0)),
            pl.BlockSpec((group, RANK, depth), lambda i: (i, 0, 0)),
        ],
        out_specs=pl.BlockSpec((RANK, group * depth), lambda i: (0, i)),
        cost_estimate=pl.CostEstimate(
            flops=6 * RANK * RANK * blocks * depth, bytes_accessed=6 * RANK * blocks * depth, transcendentals=0
        ),
        compiler_params=pltpu.CompilerParams(vmem_limit_bytes=SMALL_BYTES),
        name="row_basis",
    )(l_inv, sketch)


def ring(size, shift):
    return [(i, (i + shift) % size) for i in range(size)]


def solution(mesh):
    grid_size, tm_size = mesh.devices.shape
    fine = Mesh(mesh.devices.reshape(grid_size // 2, 2, tm_size), ("z", "c", "t"))

    def shards(anomaly, start_basis):
        points = anomaly.shape[0] * grid_size
        hours = anomaly.shape[1] * tm_size
        depth = anomaly.shape[0] // tm_size
        core = lax.axis_index("c").reshape(1).astype(jnp.int32)
        core, start_basis = lax.optimization_barrier((core, start_basis))
        a = append_basis(anomaly.reshape(tm_size, depth, anomaly.shape[1]), start_basis)
        a = lax.all_to_all(a, "t", 0, 0)
        swap = ring(2, 1)
        out, send = first_step(core, a)
        mate = lax.ppermute(send, "c", swap)
        part = lax.all_to_all(out, ("c", "t"), 0, 0)
        for step in range(ITERS):
            last = step == ITERS - 1
            if step:
                sketch = sketch_step(core, h, a, mate)
                other = lax.ppermute(sketch, "c", swap)
                out = product_step(hours, last, core, sketch, other, a, mate)
                if last:
                    rows = lax.all_gather(out[1], "t", axis=0)
                part = lax.all_to_all(out[0], "t", 0, 0)
            part = sum_step(part, grid_size // 2)
            part = lax.all_to_all(part, "z", 0, 0)
            out = hour_step(part, (2 if last else 1) * tm_size, points, last)
            h = lax.all_to_all(out[0], ("c", "t") if last else "t", 0, 0)
        home = [(i, i % 2 * tm_size + i // 2) for i in range(2 * tm_size)]
        mine = lax.ppermute(out[1], ("c", "t"), home)
        other = lax.ppermute(mine, "c", swap)
        return row_step(out[2], rows), column_step(h, mine, other, core, hours)

    return jax.shard_map(
        shards,
        mesh=fine,
        in_specs=(P(("z", "c"), "t"), P(None, "t")),
        out_specs=(P(None, ("z", "c")), P(None, "t")),
        check_vma=False,
    )
```

```python
import jax
import jax.numpy as jnp
from jax import lax
from jax.experimental import pallas as pl
from jax.experimental.pallas import tpu as pltpu
from jax.sharding import Mesh, PartitionSpec as P

ITERS = 6
RANK = 32
LANES = 128
EXTRA = RANK * RANK // LANES
ROWS = RANK + EXTRA
HEAD = 2 * RANK + 4 * EXTRA
SMALL_BYTES = 4 * 1024 * 1024
MID_BYTES = 20 * 1024 * 1024
F32 = jnp.float32
BF16 = jnp.bfloat16
HIGH = lax.Precision.HIGHEST
NT = (((1,), (1,)), ((), ()))
TN = (((0,), (0,)), ((), ()))


def split_f32(value):
    high = value.astype(BF16)
    return high, value - high.astype(F32)


def split_bf16(value):
    high, low = split_f32(value)
    return jnp.concatenate([high, low.astype(BF16)], axis=0)


def pack(gram):
    return jnp.concatenate([gram[b * EXTRA : (b + 1) * EXTRA] for b in range(RANK // EXTRA)], axis=1)


def self_gram(block, precision=None):
    return lax.dot_general(block, block, NT, precision=precision, preferred_element_type=F32)


def packed_gram(block):
    return pack(self_gram(block, HIGH))


def inverse_factor(packed, upper):
    parts = RANK // EXTRA
    shape = (EXTRA, LANES)
    lane = lax.broadcasted_iota(jnp.int32, shape, 1)
    sub = lax.broadcasted_iota(jnp.int32, shape, 0)
    work = []
    for b in range(parts):
        shift = (RANK - b * RANK) % LANES
        gram = pltpu.roll(packed, shift, 1) if shift else packed
        gram = jnp.where(lane < 2 * RANK, gram, 0.0)
        work.append(jnp.where(lane < RANK, (lane == sub + b * EXTRA).astype(F32), gram))
    scale = []
    places = range(EXTRA - 1, -1, -1) if upper else range(EXTRA)
    for block in range(parts - 1, -1, -1) if upper else range(parts):
        beyond = range(block) if upper else range(block + 1, parts)
        cols = {
            b: [jnp.broadcast_to(work[b][:, c : c + 1], shape) for c in [RANK + block * EXTRA + r for r in places]]
            for b in (block, *beyond)
        }
        rows = [jnp.broadcast_to(work[block][r : r + 1, :], shape) for r in places]
        pivots = [[jnp.broadcast_to(col[r : r + 1, :], shape) for col in cols[block]] for r in places]
        scaled = []
        final = work[block]
        diagonal = pivots[0][0]
        for i, r in enumerate(places):
            inverse = 1.0 / pivots[i][i]
            for j in range(i + 1, EXTRA):
                factor = pivots[i][j] * inverse
                for k in range(j, EXTRA):
                    pivots[j][k] = pivots[j][k] - factor * pivots[i][k]
                rows[j] = rows[j] - factor * rows[i]
                for b in beyond:
                    cols[b][j] = cols[b][j] - factor * cols[b][i]
            scaled.append(rows[i] * inverse)
            final = jnp.where(sub == r, rows[i], final)
            diagonal = jnp.where(sub == r, pivots[i][i], diagonal)
        work[block] = final
        scale.append((block, diagonal))
        for b in beyond:
            for i in range(EXTRA):
                work[b] = work[b] - cols[b][i] * scaled[i]
    rows = [work[b] / jnp.sqrt(diagonal) for b, diagonal in sorted(scale, key=lambda item: item[0])]
    return jnp.concatenate(rows, axis=0)[:, :RANK]


def append_basis(a, basis):
    blocks, depth, width = a.shape

    def kernel(a_ref, basis_ref, out_ref, sems):
        def load(t):
            return pltpu.make_async_copy(a_ref.at[t], out_ref.at[t, 0:depth, :], sems.at[t])

        for t in range(blocks):
            load(t).start()
        for t in range(blocks):
            out_ref[t, depth : depth + RANK, :] = basis_ref[...]
        for t in range(blocks):
            load(t).wait()

    return pl.pallas_call(
        kernel,
        out_shape=jax.ShapeDtypeStruct((blocks, depth + RANK, width), BF16),
        in_specs=[pl.BlockSpec(memory_space=pl.ANY), pl.BlockSpec(memory_space=pltpu.VMEM)],
        out_specs=pl.BlockSpec(memory_space=pltpu.VMEM),
        scratch_shapes=[pltpu.SemaphoreType.DMA((blocks,))],
        compiler_params=pltpu.CompilerParams(vmem_limit_bytes=MID_BYTES),
        name="append_basis",
    )(a, basis)


def first_step(a):
    blocks, depth, width = a.shape
    depth -= RANK
    half = blocks // 2

    def kernel(a_ref, out_ref, send_ref, acc, send_sems):
        def send(i):
            t = (1 - lax.axis_index("c")) * half + i
            return pltpu.make_async_copy(a_ref.at[t, 0:depth, :], send_ref.at[i], send_sems.at[i])

        for i in range(half):
            send(i).start()
        for t in range(blocks):
            basis = a_ref[t, depth : depth + RANK, :]
            term = lax.dot_general(basis, a_ref[t, 0:depth, :], NT, preferred_element_type=F32)
            if t == 0:
                acc[...] = term
            else:
                acc[...] += term
        sketch = acc[...]
        gram = packed_gram(sketch)
        left = split_bf16(sketch)
        for t in range(blocks):
            both = jnp.dot(left, a_ref[t, 0:depth, :], preferred_element_type=F32)
            store_part(out_ref, t, both[0:RANK] + both[RANK : 2 * RANK], gram)
        for i in range(half):
            send(i).wait()

    return pl.pallas_call(
        kernel,
        out_shape=[
            jax.ShapeDtypeStruct((2 * blocks, ROWS, LANES), F32),
            jax.ShapeDtypeStruct((half, depth, width), BF16),
        ],
        in_specs=[pl.BlockSpec(memory_space=pltpu.VMEM)],
        out_specs=[pl.BlockSpec(memory_space=pltpu.VMEM), pl.BlockSpec(memory_space=pl.ANY)],
        scratch_shapes=[pltpu.VMEM((RANK, depth), F32), pltpu.SemaphoreType.DMA((half,))],
        compiler_params=pltpu.CompilerParams(vmem_limit_bytes=MID_BYTES),
        name="first_products",
    )(a)


def store_part(out_ref, block, part, gram):
    for side in range(2):
        out_ref[2 * block + side, 0:RANK, :] = part[:, side * LANES : (side + 1) * LANES]
        out_ref[2 * block + side, RANK:ROWS, :] = gram


def sketch_step(h, a, mate):
    half, depth, width = mate.shape

    def kernel(h_ref, a_ref, mate_ref, out_ref):
        parts = [jnp.concatenate([h_ref[2 * i], h_ref[2 * i + 1]], axis=1) for i in range(half)]
        for side in range(2):
            rows = slice(side * RANK, (side + 1) * RANK)
            for i in range(half):
                block = mate_ref[i] if side else a_ref[lax.axis_index("c") * half + i, 0:depth, :]
                term = lax.dot_general(parts[i], block, NT, preferred_element_type=F32)
                if i == 0:
                    out_ref[rows, :] = term
                else:
                    out_ref[rows, :] += term
        whole = jnp.concatenate(parts, axis=1)
        out_ref[2 * RANK :, :] = jnp.zeros((EXTRA, depth), F32)
        out_ref[2 * RANK :, 0:LANES] = pack(self_gram(whole))

    return pl.pallas_call(
        kernel,
        out_shape=jax.ShapeDtypeStruct((2 * RANK + EXTRA, depth), F32),
        in_specs=[
            pl.BlockSpec(memory_space=pltpu.VMEM),
            pl.BlockSpec(memory_space=pltpu.VMEM),
            pl.BlockSpec(memory_space=pltpu.VMEM),
        ],
        out_specs=pl.BlockSpec(memory_space=pltpu.VMEM),
        compiler_params=pltpu.CompilerParams(vmem_limit_bytes=MID_BYTES),
        name="partial_sketch",
    )(h, a, mate)


def product_step(hours, keep, mine, other, a, mate):
    half, depth, width = mate.shape

    def kernel(mine_ref, other_ref, a_ref, mate_ref, out_ref):
        gram = mine_ref[2 * RANK :, 0:LANES] + other_ref[2 * RANK :, 0:LANES]
        v_inv = inverse_factor(gram, True) * float(hours) ** 0.5
        own = mine_ref[0:RANK, :] + other_ref[RANK : 2 * RANK, :]
        own = jnp.dot(v_inv, own, precision=HIGH, preferred_element_type=F32)
        far = mine_ref[RANK : 2 * RANK, :] + other_ref[0:RANK, :]
        far = jnp.dot(v_inv, far, precision=HIGH, preferred_element_type=F32)
        gram = pack(self_gram(own, HIGH) + self_gram(far, HIGH))
        left = split_bf16(own)
        right = split_bf16(far)
        if keep:
            high, low = split_f32(gram)
            rest = split_bf16(low)
            gram = jnp.concatenate([high, rest, jnp.zeros((EXTRA, LANES), BF16)], axis=0)
            kept = own.astype(BF16)
        for i in range(half):
            both = jnp.dot(left, a_ref[lax.axis_index("c") * half + i, 0:depth, :], preferred_element_type=F32)
            both = both + jnp.dot(right, mate_ref[i], preferred_element_type=F32)
            part = both[0:RANK] + both[RANK : 2 * RANK]
            if not keep:
                store_part(out_ref, i, part, gram)
                continue
            for side in range(2):
                k = 2 * i + side
                out_ref[k, 0 : 2 * RANK, :] = split_bf16(part[:, side * LANES : (side + 1) * LANES])
                out_ref[k, 2 * RANK : HEAD, :] = gram
                for j in range(depth // LANES):
                    out_ref[k, HEAD + j * RANK : HEAD + (j + 1) * RANK, :] = kept[:, j * LANES : (j + 1) * LANES]

    out_shape = jax.ShapeDtypeStruct((2 * half, ROWS, LANES), F32)
    if keep:
        out_shape = jax.ShapeDtypeStruct((2 * half, HEAD + RANK * depth // LANES, LANES), BF16)
    return pl.pallas_call(
        kernel,
        out_shape=out_shape,
        in_specs=[
            pl.BlockSpec(memory_space=pltpu.VMEM),
            pl.BlockSpec(memory_space=pltpu.VMEM),
            pl.BlockSpec(memory_space=pltpu.VMEM),
            pl.BlockSpec(memory_space=pltpu.VMEM),
        ],
        out_specs=pl.BlockSpec(memory_space=pltpu.VMEM),
        compiler_params=pltpu.CompilerParams(vmem_limit_bytes=MID_BYTES),
        name="hour_products",
    )(mine, other, a, mate)


def sum_step(parts, copies):
    plain = parts.dtype == F32

    def kernel(in_ref, out_ref):
        total = in_ref[0] if plain else in_ref[0, 0:HEAD, :].astype(F32)
        for k in range(1, parts.shape[0]):
            total = total + (in_ref[k] if plain else in_ref[k, 0:HEAD, :].astype(F32))
        if not plain:
            products = total[0:RANK] + total[RANK : 2 * RANK]
            gram = [total[2 * RANK + p * EXTRA : 2 * RANK + (p + 1) * EXTRA] for p in range(3)]
            total = jnp.concatenate([products, gram[0] + (gram[1] + gram[2])], axis=0)
        for k in range(copies):
            out_ref[k] = total

    return pl.pallas_call(
        kernel,
        out_shape=jax.ShapeDtypeStruct((copies, ROWS, LANES), F32),
        in_specs=[pl.BlockSpec(memory_space=pltpu.VMEM)],
        out_specs=pl.BlockSpec(memory_space=pltpu.VMEM),
        compiler_params=pltpu.CompilerParams(vmem_limit_bytes=SMALL_BYTES),
        name="sum_parts",
    )(parts)


def hour_step(parts, copies, points, last):
    def kernel(in_ref, *outs):
        total = in_ref[0]
        for k in range(1, parts.shape[0]):
            total = total + in_ref[k]
        l_inv = inverse_factor(total[RANK:ROWS], False) * float(points) ** 0.5
        hours = jnp.dot(l_inv, total[0:RANK], precision=HIGH, preferred_element_type=F32)
        hours = lax.dot_general(l_inv, hours, TN, precision=HIGH, preferred_element_type=F32)
        if last:
            gram = packed_gram(hours)
            for k in range(copies):
                outs[0][k] = gram
            outs[1][...] = hours
            outs[2][...] = l_inv
        else:
            rounded = hours.astype(BF16)
            for k in range(copies):
                outs[0][k] = rounded

    out_shape = [jax.ShapeDtypeStruct((copies, RANK, LANES), BF16)]
    if last:
        out_shape = [
            jax.ShapeDtypeStruct((copies, EXTRA, LANES), F32),
            jax.ShapeDtypeStruct((RANK, LANES), F32),
            jax.ShapeDtypeStruct((RANK, RANK), F32),
        ]
    return pl.pallas_call(
        kernel,
        out_shape=out_shape,
        in_specs=[pl.BlockSpec(memory_space=pltpu.VMEM)],
        out_specs=[pl.BlockSpec(memory_space=pltpu.VMEM)] * len(out_shape),
        compiler_params=pltpu.CompilerParams(vmem_limit_bytes=SMALL_BYTES),
        name="row_factor",
    )(parts)


def column_step(grams, mine, other, hours):
    def kernel(gram_ref, mine_ref, other_ref, out_ref):
        total = gram_ref[0]
        for k in range(1, grams.shape[0]):
            total = total + gram_ref[k]
        v_inv = inverse_factor(total, True) * float(hours) ** 0.5
        first = lax.axis_index("c") == 0
        low = jnp.where(first, mine_ref[...], other_ref[...])
        high = jnp.where(first, other_ref[...], mine_ref[...])
        block = jnp.concatenate([low, high], axis=1)
        out_ref[...] = jnp.dot(v_inv, block, precision=HIGH, preferred_element_type=F32)

    return pl.pallas_call(
        kernel,
        out_shape=jax.ShapeDtypeStruct((RANK, 2 * LANES), F32),
        in_specs=[pl.BlockSpec(memory_space=pltpu.VMEM)] * 3,
        out_specs=pl.BlockSpec(memory_space=pltpu.VMEM),
        compiler_params=pltpu.CompilerParams(vmem_limit_bytes=SMALL_BYTES),
        name="column_factor",
    )(grams, mine, other)


def row_step(l_inv, parts):
    blocks, height, _ = parts.shape
    pieces = (height - HEAD) // RANK
    depth = pieces * LANES
    group = 4

    def kernel(l_ref, s_ref, out_ref):
        left = split_bf16(l_ref[...])
        for k in range(group):
            rows = [s_ref[k, HEAD + j * RANK : HEAD + (j + 1) * RANK, :] for j in range(pieces)]
            out = jnp.dot(left, jnp.concatenate(rows, axis=1), preferred_element_type=F32)
            out_ref[:, k * depth : (k + 1) * depth] = out[0:RANK] + out[RANK : 2 * RANK]

    return pl.pallas_call(
        kernel,
        grid=(blocks // group,),
        out_shape=jax.ShapeDtypeStruct((RANK, blocks * depth), F32),
        in_specs=[
            pl.BlockSpec((RANK, RANK), lambda i: (0, 0)),
            pl.BlockSpec((group, height, LANES), lambda i: (i, 0, 0)),
        ],
        out_specs=pl.BlockSpec((RANK, group * depth), lambda i: (0, i)),
        cost_estimate=pl.CostEstimate(
            flops=4 * RANK * RANK * blocks * depth, bytes_accessed=6 * RANK * blocks * depth, transcendentals=0
        ),
        compiler_params=pltpu.CompilerParams(vmem_limit_bytes=SMALL_BYTES),
        name="row_basis",
    )(l_inv, parts)


def ring(size, shift):
    return [(i, (i + shift) % size) for i in range(size)]


def solution(mesh):
    grid_size, tm_size = mesh.devices.shape
    fine = Mesh(mesh.devices.reshape(grid_size // 2, 2, tm_size), ("z", "c", "t"))

    def shards(anomaly, start_basis):
        points = anomaly.shape[0] * grid_size
        hours = anomaly.shape[1] * tm_size
        depth = anomaly.shape[0] // tm_size
        a = append_basis(anomaly.reshape(tm_size, depth, anomaly.shape[1]), start_basis)
        a = lax.all_to_all(a, "t", 0, 0)
        swap = ring(2, 1)
        out, send = first_step(a)
        mate = lax.ppermute(send, "c", swap)
        part = lax.all_to_all(out, ("c", "t"), 0, 0)
        for step in range(ITERS):
            last = step == ITERS - 1
            if step:
                sketch = sketch_step(h, a, mate)
                other = lax.ppermute(sketch, "c", swap)
                out = product_step(hours, last, sketch, other, a, mate)
                part = lax.all_to_all(out, "t", 0, 0)
                if last:
                    rows = part
            part = sum_step(part, grid_size // 2)
            part = lax.all_to_all(part, "z", 0, 0)
            out = hour_step(part, (2 if last else 1) * tm_size, points, last)
            h = lax.all_to_all(out[0], ("c", "t") if last else "t", 0, 0)
        home = [(i, i % 2 * tm_size + i // 2) for i in range(2 * tm_size)]
        mine = lax.ppermute(out[1], ("c", "t"), home)
        other = lax.ppermute(mine, "c", swap)
        return row_step(out[2], rows), column_step(h, mine, other, hours)

    return jax.shard_map(
        shards,
        mesh=fine,
        in_specs=(P(("z", "c"), "t"), P(None, "t")),
        out_specs=(P(None, ("z", "c")), P(None, "t")),
        check_vma=False,
    )
```

```python
import jax
import jax.numpy as jnp
from jax import lax
from jax.experimental import pallas as pl
from jax.experimental.pallas import tpu as pltpu
from jax.sharding import Mesh, PartitionSpec as P

ITERS = 6
RANK = 32
LANES = 128
EXTRA = RANK * RANK // LANES
ROWS = RANK + EXTRA
NARROW = RANK + 2 * EXTRA
HEAD = 2 * RANK + 4 * EXTRA
SMALL_BYTES = 4 * 1024 * 1024
MID_BYTES = 20 * 1024 * 1024
F32 = jnp.float32
BF16 = jnp.bfloat16
HIGH = lax.Precision.HIGHEST
NT = (((1,), (1,)), ((), ()))
TN = (((0,), (0,)), ((), ()))


def split_f32(value):
    high = value.astype(BF16)
    return high, value - high.astype(F32)


def split_bf16(value):
    high, low = split_f32(value)
    return jnp.concatenate([high, low.astype(BF16)], axis=0)


def pack(gram):
    return jnp.concatenate([gram[b * EXTRA : (b + 1) * EXTRA] for b in range(RANK // EXTRA)], axis=1)


def self_gram(block, precision=None):
    return lax.dot_general(block, block, NT, precision=precision, preferred_element_type=F32)


def packed_gram(block):
    return pack(self_gram(block, HIGH))


def inverse_factor(packed, upper):
    parts = RANK // EXTRA
    shape = (EXTRA, LANES)
    lane = lax.broadcasted_iota(jnp.int32, shape, 1)
    sub = lax.broadcasted_iota(jnp.int32, shape, 0)
    work = []
    for b in range(parts):
        shift = (RANK - b * RANK) % LANES
        gram = pltpu.roll(packed, shift, 1) if shift else packed
        gram = jnp.where(lane < 2 * RANK, gram, 0.0)
        work.append(jnp.where(lane < RANK, (lane == sub + b * EXTRA).astype(F32), gram))
    scale = []
    places = range(EXTRA - 1, -1, -1) if upper else range(EXTRA)
    for block in range(parts - 1, -1, -1) if upper else range(parts):
        beyond = range(block) if upper else range(block + 1, parts)
        cols = {
            b: [jnp.broadcast_to(work[b][:, c : c + 1], shape) for c in [RANK + block * EXTRA + r for r in places]]
            for b in (block, *beyond)
        }
        rows = [jnp.broadcast_to(work[block][r : r + 1, :], shape) for r in places]
        pivots = [[jnp.broadcast_to(col[r : r + 1, :], shape) for col in cols[block]] for r in places]
        scaled = []
        final = work[block]
        diagonal = pivots[0][0]
        for i, r in enumerate(places):
            inverse = 1.0 / pivots[i][i]
            for j in range(i + 1, EXTRA):
                factor = pivots[i][j] * inverse
                for k in range(j, EXTRA):
                    pivots[j][k] = pivots[j][k] - factor * pivots[i][k]
                rows[j] = rows[j] - factor * rows[i]
                for b in beyond:
                    cols[b][j] = cols[b][j] - factor * cols[b][i]
            scaled.append(rows[i] * inverse)
            final = jnp.where(sub == r, rows[i], final)
            diagonal = jnp.where(sub == r, pivots[i][i], diagonal)
        work[block] = final
        scale.append((block, diagonal))
        for b in beyond:
            for i in range(EXTRA):
                work[b] = work[b] - cols[b][i] * scaled[i]
    rows = [work[b] / jnp.sqrt(diagonal) for b, diagonal in sorted(scale, key=lambda item: item[0])]
    return jnp.concatenate(rows, axis=0)[:, :RANK]


def append_basis(a, basis):
    blocks, depth, width = a.shape

    def kernel(a_ref, basis_ref, out_ref, sems):
        def load(t):
            return pltpu.make_async_copy(a_ref.at[t], out_ref.at[t, 0:depth, :], sems.at[t])

        for t in range(blocks):
            load(t).start()
        for t in range(blocks):
            out_ref[t, depth : depth + RANK, :] = basis_ref[...]
        for t in range(blocks):
            load(t).wait()

    return pl.pallas_call(
        kernel,
        out_shape=jax.ShapeDtypeStruct((blocks, depth + RANK, width), BF16),
        in_specs=[pl.BlockSpec(memory_space=pl.ANY), pl.BlockSpec(memory_space=pltpu.VMEM)],
        out_specs=pl.BlockSpec(memory_space=pltpu.VMEM),
        scratch_shapes=[pltpu.SemaphoreType.DMA((blocks,))],
        compiler_params=pltpu.CompilerParams(vmem_limit_bytes=MID_BYTES),
        name="append_basis",
    )(a, basis)


def first_step(a):
    blocks, depth, width = a.shape
    depth -= RANK
    half = blocks // 2

    def kernel(a_ref, out_ref, send_ref, acc, send_sems):
        def send(i):
            t = (1 - lax.axis_index("c")) * half + i
            return pltpu.make_async_copy(a_ref.at[t, 0:depth, :], send_ref.at[i], send_sems.at[i])

        for i in range(half):
            send(i).start()
        for t in range(blocks):
            basis = a_ref[t, depth : depth + RANK, :]
            term = lax.dot_general(basis, a_ref[t, 0:depth, :], NT, preferred_element_type=F32)
            if t == 0:
                acc[...] = term
            else:
                acc[...] += term
        sketch = acc[...]
        gram = packed_gram(sketch)
        left = split_bf16(sketch)
        for t in range(blocks):
            both = jnp.dot(left, a_ref[t, 0:depth, :], preferred_element_type=F32)
            store_part(out_ref, t, both[0:RANK] + both[RANK : 2 * RANK], gram)
        for i in range(half):
            send(i).wait()

    return pl.pallas_call(
        kernel,
        out_shape=[
            jax.ShapeDtypeStruct((2 * blocks, ROWS, LANES), F32),
            jax.ShapeDtypeStruct((half, depth, width), BF16),
        ],
        in_specs=[pl.BlockSpec(memory_space=pltpu.VMEM)],
        out_specs=[pl.BlockSpec(memory_space=pltpu.VMEM), pl.BlockSpec(memory_space=pl.ANY)],
        scratch_shapes=[pltpu.VMEM((RANK, depth), F32), pltpu.SemaphoreType.DMA((half,))],
        compiler_params=pltpu.CompilerParams(vmem_limit_bytes=MID_BYTES),
        name="first_products",
    )(a)


def store_part(out_ref, block, part, gram):
    for side in range(2):
        out_ref[2 * block + side, 0:RANK, :] = part[:, side * LANES : (side + 1) * LANES]
        out_ref[2 * block + side, RANK:ROWS, :] = gram


def sketch_step(h, a, mate):
    half, depth, width = mate.shape

    def kernel(h_ref, a_ref, mate_ref, out_ref):
        parts = [jnp.concatenate([h_ref[2 * i], h_ref[2 * i + 1]], axis=1) for i in range(half)]
        for side in range(2):
            rows = slice(side * RANK, (side + 1) * RANK)
            for i in range(half):
                block = mate_ref[i] if side else a_ref[lax.axis_index("c") * half + i, 0:depth, :]
                term = lax.dot_general(parts[i], block, NT, preferred_element_type=F32)
                if i == 0:
                    out_ref[rows, :] = term
                else:
                    out_ref[rows, :] += term
        whole = jnp.concatenate(parts, axis=1)
        out_ref[2 * RANK :, :] = jnp.zeros((EXTRA, depth), F32)
        out_ref[2 * RANK :, 0:LANES] = pack(self_gram(whole))

    return pl.pallas_call(
        kernel,
        out_shape=jax.ShapeDtypeStruct((2 * RANK + EXTRA, depth), F32),
        in_specs=[
            pl.BlockSpec(memory_space=pltpu.VMEM),
            pl.BlockSpec(memory_space=pltpu.VMEM),
            pl.BlockSpec(memory_space=pltpu.VMEM),
        ],
        out_specs=pl.BlockSpec(memory_space=pltpu.VMEM),
        compiler_params=pltpu.CompilerParams(vmem_limit_bytes=MID_BYTES),
        name="partial_sketch",
    )(h, a, mate)


def product_step(hours, keep, mine, other, a, mate, l_inv=None):
    half, depth, width = mate.shape
    narrow = l_inv is not None
    operands = (mine, other, a, mate) + ((l_inv,) if narrow else ())

    def kernel(mine_ref, other_ref, a_ref, mate_ref, *rest_refs):
        out_ref = rest_refs[-1]
        gram = mine_ref[2 * RANK :, 0:LANES] + other_ref[2 * RANK :, 0:LANES]
        v_inv = inverse_factor(gram, True) * float(hours) ** 0.5
        if narrow:
            v_inv = jnp.dot(rest_refs[0][...], v_inv, precision=HIGH, preferred_element_type=F32)
        own = mine_ref[0:RANK, :] + other_ref[RANK : 2 * RANK, :]
        own = jnp.dot(v_inv, own, precision=HIGH, preferred_element_type=F32)
        far = mine_ref[RANK : 2 * RANK, :] + other_ref[0:RANK, :]
        far = jnp.dot(v_inv, far, precision=HIGH, preferred_element_type=F32)
        gram = pack(self_gram(own, HIGH) + self_gram(far, HIGH))
        left = split_bf16(own)
        right = split_bf16(far)
        if keep:
            high, low = split_f32(gram)
            rest = split_bf16(low)
            gram = jnp.concatenate([high, rest, jnp.zeros((EXTRA, LANES), BF16)], axis=0)
            kept = own.astype(BF16)
        for i in range(half):
            both = jnp.dot(left, a_ref[lax.axis_index("c") * half + i, 0:depth, :], preferred_element_type=F32)
            both = both + jnp.dot(right, mate_ref[i], preferred_element_type=F32)
            part = both[0:RANK] + both[RANK : 2 * RANK]
            if narrow:
                for side in range(2):
                    k = 2 * i + side
                    out_ref[k, 0:RANK, :] = part[:, side * LANES : (side + 1) * LANES].astype(BF16)
                    out_ref[k, RANK:NARROW, :] = split_bf16(gram)
                continue
            if not keep:
                store_part(out_ref, i, part, gram)
                continue
            for side in range(2):
                k = 2 * i + side
                out_ref[k, 0 : 2 * RANK, :] = split_bf16(part[:, side * LANES : (side + 1) * LANES])
                out_ref[k, 2 * RANK : HEAD, :] = gram
                for j in range(depth // LANES):
                    out_ref[k, HEAD + j * RANK : HEAD + (j + 1) * RANK, :] = kept[:, j * LANES : (j + 1) * LANES]

    out_shape = jax.ShapeDtypeStruct((2 * half, ROWS, LANES), F32)
    if keep:
        out_shape = jax.ShapeDtypeStruct((2 * half, HEAD + RANK * depth // LANES, LANES), BF16)
    if narrow:
        out_shape = jax.ShapeDtypeStruct((2 * half, NARROW, LANES), BF16)
    return pl.pallas_call(
        kernel,
        out_shape=out_shape,
        in_specs=[pl.BlockSpec(memory_space=pltpu.VMEM)] * len(operands),
        out_specs=pl.BlockSpec(memory_space=pltpu.VMEM),
        compiler_params=pltpu.CompilerParams(vmem_limit_bytes=MID_BYTES),
        name="hour_products",
    )(*operands)


def widen(total):
    if total.shape[0] == NARROW:
        return jnp.concatenate([total[0:RANK], total[RANK:ROWS] + total[ROWS:NARROW]], axis=0)
    products = total[0:RANK] + total[RANK : 2 * RANK]
    gram = [total[2 * RANK + p * EXTRA : 2 * RANK + (p + 1) * EXTRA] for p in range(3)]
    return jnp.concatenate([products, gram[0] + (gram[1] + gram[2])], axis=0)


def sum_parts(ref):
    rows = min(ref.shape[1], HEAD)
    total = ref[0, 0:rows, :].astype(F32)
    for k in range(1, ref.shape[0]):
        total = total + ref[k, 0:rows, :].astype(F32)
    return total if ref.dtype == F32 else widen(total)


def sum_step(parts, copies):
    narrow = parts.shape[1] == NARROW

    def kernel(in_ref, out_ref):
        total = sum_parts(in_ref)
        if narrow:
            total = jnp.concatenate([total[0:RANK].astype(BF16), split_bf16(total[RANK:ROWS])], axis=0)
        for k in range(copies):
            out_ref[k] = total

    return pl.pallas_call(
        kernel,
        out_shape=jax.ShapeDtypeStruct(
            (copies, NARROW if narrow else ROWS, LANES), BF16 if narrow else F32
        ),
        in_specs=[pl.BlockSpec(memory_space=pltpu.VMEM)],
        out_specs=pl.BlockSpec(memory_space=pltpu.VMEM),
        compiler_params=pltpu.CompilerParams(vmem_limit_bytes=SMALL_BYTES),
        name="sum_parts",
    )(parts)


def hour_step(parts, copies, points, last, l_prev=None):
    operands = (parts,) if l_prev is None else (parts, l_prev)

    def kernel(in_ref, *refs):
        outs = refs[len(operands) - 1 :]
        total = sum_parts(in_ref)
        l_inv = inverse_factor(total[RANK:ROWS], False) * float(points) ** 0.5
        hours = jnp.dot(l_inv, total[0:RANK], precision=HIGH, preferred_element_type=F32)
        if l_prev is not None:
            l_inv = jnp.dot(l_inv, refs[0][...], precision=HIGH, preferred_element_type=F32)
        outs[1][...] = l_inv
        hours = lax.dot_general(l_inv, hours, TN, precision=HIGH, preferred_element_type=F32)
        if last:
            gram = packed_gram(hours)
            for k in range(copies):
                outs[0][k] = gram
            outs[2][...] = hours
        else:
            rounded = hours.astype(BF16)
            for k in range(copies):
                outs[0][k] = rounded

    out_shape = [
        jax.ShapeDtypeStruct((copies, EXTRA, LANES), F32) if last else jax.ShapeDtypeStruct((copies, RANK, LANES), BF16),
        jax.ShapeDtypeStruct((RANK, RANK), F32),
    ]
    if last:
        out_shape.append(jax.ShapeDtypeStruct((RANK, LANES), F32))
    return pl.pallas_call(
        kernel,
        out_shape=out_shape,
        in_specs=[pl.BlockSpec(memory_space=pltpu.VMEM)] * len(operands),
        out_specs=[pl.BlockSpec(memory_space=pltpu.VMEM)] * len(out_shape),
        compiler_params=pltpu.CompilerParams(vmem_limit_bytes=SMALL_BYTES),
        name="row_factor",
    )(*operands)


def column_step(grams, mine, other, hours):
    def kernel(gram_ref, mine_ref, other_ref, out_ref):
        total = gram_ref[0]
        for k in range(1, grams.shape[0]):
            total = total + gram_ref[k]
        v_inv = inverse_factor(total, True) * float(hours) ** 0.5
        first = lax.axis_index("c") == 0
        low = jnp.where(first, mine_ref[...], other_ref[...])
        high = jnp.where(first, other_ref[...], mine_ref[...])
        block = jnp.concatenate([low, high], axis=1)
        out_ref[...] = jnp.dot(v_inv, block, precision=HIGH, preferred_element_type=F32)

    return pl.pallas_call(
        kernel,
        out_shape=jax.ShapeDtypeStruct((RANK, 2 * LANES), F32),
        in_specs=[pl.BlockSpec(memory_space=pltpu.VMEM)] * 3,
        out_specs=pl.BlockSpec(memory_space=pltpu.VMEM),
        compiler_params=pltpu.CompilerParams(vmem_limit_bytes=SMALL_BYTES),
        name="column_factor",
    )(grams, mine, other)


def row_step(l_inv, parts):
    blocks, height, _ = parts.shape
    pieces = (height - HEAD) // RANK
    depth = pieces * LANES
    group = 4

    def kernel(l_ref, s_ref, out_ref):
        left = split_bf16(l_ref[...])
        for k in range(group):
            rows = [s_ref[k, HEAD + j * RANK : HEAD + (j + 1) * RANK, :] for j in range(pieces)]
            out = jnp.dot(left, jnp.concatenate(rows, axis=1), preferred_element_type=F32)
            out_ref[:, k * depth : (k + 1) * depth] = out[0:RANK] + out[RANK : 2 * RANK]

    return pl.pallas_call(
        kernel,
        grid=(blocks // group,),
        out_shape=jax.ShapeDtypeStruct((RANK, blocks * depth), F32),
        in_specs=[
            pl.BlockSpec((RANK, RANK), lambda i: (0, 0)),
            pl.BlockSpec((group, height, LANES), lambda i: (i, 0, 0)),
        ],
        out_specs=pl.BlockSpec((RANK, group * depth), lambda i: (0, i)),
        cost_estimate=pl.CostEstimate(
            flops=4 * RANK * RANK * blocks * depth, bytes_accessed=6 * RANK * blocks * depth, transcendentals=0
        ),
        compiler_params=pltpu.CompilerParams(vmem_limit_bytes=SMALL_BYTES),
        name="row_basis",
    )(l_inv, parts)


def ring(size, shift):
    return [(i, (i + shift) % size) for i in range(size)]


def solution(mesh):
    grid_size, tm_size = mesh.devices.shape
    fine = Mesh(mesh.devices.reshape(grid_size // 2, 2, tm_size), ("z", "c", "t"))

    def shards(anomaly, start_basis):
        points = anomaly.shape[0] * grid_size
        hours = anomaly.shape[1] * tm_size
        depth = anomaly.shape[0] // tm_size
        a = append_basis(anomaly.reshape(tm_size, depth, anomaly.shape[1]), start_basis)
        a = lax.all_to_all(a, "t", 0, 0)
        swap = ring(2, 1)
        out, send = first_step(a)
        mate = lax.ppermute(send, "c", swap)
        part = lax.all_to_all(out, ("c", "t"), 0, 0)
        for step in range(ITERS):
            last = step == ITERS - 1
            l_prev = l_inv if 1 < step < ITERS - 1 else None
            if step:
                sketch = sketch_step(h, a, mate)
                other = lax.ppermute(sketch, "c", swap)
                out = product_step(hours, last, sketch, other, a, mate, l_prev)
                part = lax.all_to_all(out, "t", 0, 0)
                if last:
                    rows = part
            part = sum_step(part, grid_size // 2)
            part = lax.all_to_all(part, "z", 0, 0)
            h, l_inv, *whole = hour_step(part, (2 if last else 1) * tm_size, points, last, l_prev)
            h = lax.all_to_all(h, ("c", "t") if last else "t", 0, 0)
        home = [(i, i % 2 * tm_size + i // 2) for i in range(2 * tm_size)]
        mine = lax.ppermute(whole[0], ("c", "t"), home)
        other = lax.ppermute(mine, "c", swap)
        return row_step(l_inv, rows), column_step(h, mine, other, hours)

    return jax.shard_map(
        shards,
        mesh=fine,
        in_specs=(P(("z", "c"), "t"), P(None, "t")),
        out_specs=(P(None, ("z", "c")), P(None, "t")),
        check_vma=False,
    )
```

```python
import jax
import jax.numpy as jnp
from jax import lax
from jax.experimental import pallas as pl
from jax.experimental.pallas import tpu as pltpu
from jax.sharding import Mesh, PartitionSpec as P

ITERS = 6
RANK = 32
LANES = 128
EXTRA = RANK * RANK // LANES
ROWS = RANK + EXTRA
NARROW = RANK + 2 * EXTRA
SMALL_BYTES = 4 * 1024 * 1024
MID_BYTES = 20 * 1024 * 1024
F32 = jnp.float32
BF16 = jnp.bfloat16
HIGH = lax.Precision.HIGHEST
NT = (((1,), (1,)), ((), ()))
TN = (((0,), (0,)), ((), ()))


def split_f32(value):
    high = value.astype(BF16)
    return high, value - high.astype(F32)


def split_bf16(value):
    high, low = split_f32(value)
    return jnp.concatenate([high, low.astype(BF16)], axis=0)


def pack(gram):
    return jnp.concatenate([gram[b * EXTRA : (b + 1) * EXTRA] for b in range(RANK // EXTRA)], axis=1)


def self_gram(block, precision=None):
    return lax.dot_general(block, block, NT, precision=precision, preferred_element_type=F32)


def packed_gram(block):
    return pack(self_gram(block, HIGH))


def inverse_factor(packed, upper):
    parts = RANK // EXTRA
    shape = (EXTRA, LANES)
    lane = lax.broadcasted_iota(jnp.int32, shape, 1)
    sub = lax.broadcasted_iota(jnp.int32, shape, 0)
    work = []
    for b in range(parts):
        shift = (RANK - b * RANK) % LANES
        gram = pltpu.roll(packed, shift, 1) if shift else packed
        gram = jnp.where(lane < 2 * RANK, gram, 0.0)
        work.append(jnp.where(lane < RANK, (lane == sub + b * EXTRA).astype(F32), gram))
    scale = []
    places = range(EXTRA - 1, -1, -1) if upper else range(EXTRA)
    for block in range(parts - 1, -1, -1) if upper else range(parts):
        beyond = range(block) if upper else range(block + 1, parts)
        cols = {
            b: [jnp.broadcast_to(work[b][:, c : c + 1], shape) for c in [RANK + block * EXTRA + r for r in places]]
            for b in (block, *beyond)
        }
        rows = [jnp.broadcast_to(work[block][r : r + 1, :], shape) for r in places]
        pivots = [[jnp.broadcast_to(col[r : r + 1, :], shape) for col in cols[block]] for r in places]
        scaled = []
        final = work[block]
        diagonal = pivots[0][0]
        for i, r in enumerate(places):
            inverse = 1.0 / pivots[i][i]
            for j in range(i + 1, EXTRA):
                factor = pivots[i][j] * inverse
                for k in range(j, EXTRA):
                    pivots[j][k] = pivots[j][k] - factor * pivots[i][k]
                rows[j] = rows[j] - factor * rows[i]
                for b in beyond:
                    cols[b][j] = cols[b][j] - factor * cols[b][i]
            scaled.append(rows[i] * inverse)
            final = jnp.where(sub == r, rows[i], final)
            diagonal = jnp.where(sub == r, pivots[i][i], diagonal)
        work[block] = final
        scale.append((block, diagonal))
        for b in beyond:
            for i in range(EXTRA):
                work[b] = work[b] - cols[b][i] * scaled[i]
    rows = [work[b] / jnp.sqrt(diagonal) for b, diagonal in sorted(scale, key=lambda item: item[0])]
    return jnp.concatenate(rows, axis=0)[:, :RANK]


def append_basis(a, basis):
    blocks, depth, width = a.shape

    def kernel(a_ref, basis_ref, out_ref, sems):
        def load(t):
            return pltpu.make_async_copy(a_ref.at[t], out_ref.at[t, 0:depth, :], sems.at[t])

        for t in range(blocks):
            load(t).start()
        for t in range(blocks):
            out_ref[t, depth : depth + RANK, :] = basis_ref[...]
        for t in range(blocks):
            load(t).wait()

    return pl.pallas_call(
        kernel,
        out_shape=jax.ShapeDtypeStruct((blocks, depth + RANK, width), BF16),
        in_specs=[pl.BlockSpec(memory_space=pl.ANY), pl.BlockSpec(memory_space=pltpu.VMEM)],
        out_specs=pl.BlockSpec(memory_space=pltpu.VMEM),
        scratch_shapes=[pltpu.SemaphoreType.DMA((blocks,))],
        compiler_params=pltpu.CompilerParams(vmem_limit_bytes=MID_BYTES),
        name="append_basis",
    )(a, basis)


def first_step(a):
    blocks, depth, width = a.shape
    depth -= RANK
    half = blocks // 2

    def kernel(a_ref, out_ref, send_ref, acc, send_sems):
        def send(i):
            t = (1 - lax.axis_index("c")) * half + i
            return pltpu.make_async_copy(a_ref.at[t, 0:depth, :], send_ref.at[i], send_sems.at[i])

        for i in range(half):
            send(i).start()
        for t in range(blocks):
            basis = a_ref[t, depth : depth + RANK, :]
            term = lax.dot_general(basis, a_ref[t, 0:depth, :], NT, preferred_element_type=F32)
            if t == 0:
                acc[...] = term
            else:
                acc[...] += term
        sketch = acc[...]
        gram = packed_gram(sketch)
        left = split_bf16(sketch)
        for t in range(blocks):
            both = jnp.dot(left, a_ref[t, 0:depth, :], preferred_element_type=F32)
            store_part(out_ref, t, both[0:RANK] + both[RANK : 2 * RANK], gram)
        for i in range(half):
            send(i).wait()

    return pl.pallas_call(
        kernel,
        out_shape=[
            jax.ShapeDtypeStruct((2 * blocks, ROWS, LANES), F32),
            jax.ShapeDtypeStruct((half, depth, width), BF16),
        ],
        in_specs=[pl.BlockSpec(memory_space=pltpu.VMEM)],
        out_specs=[pl.BlockSpec(memory_space=pltpu.VMEM), pl.BlockSpec(memory_space=pl.ANY)],
        scratch_shapes=[pltpu.VMEM((RANK, depth), F32), pltpu.SemaphoreType.DMA((half,))],
        compiler_params=pltpu.CompilerParams(vmem_limit_bytes=MID_BYTES),
        name="first_products",
    )(a)


def store_part(out_ref, block, part, gram):
    for side in range(2):
        out_ref[2 * block + side, 0:RANK, :] = part[:, side * LANES : (side + 1) * LANES]
        out_ref[2 * block + side, RANK:ROWS, :] = gram


def sketch_step(h, a, mate):
    half, depth, width = mate.shape

    def kernel(h_ref, a_ref, mate_ref, out_ref):
        parts = [jnp.concatenate([h_ref[2 * i], h_ref[2 * i + 1]], axis=1) for i in range(half)]
        for side in range(2):
            rows = slice(side * RANK, (side + 1) * RANK)
            for i in range(half):
                block = mate_ref[i] if side else a_ref[lax.axis_index("c") * half + i, 0:depth, :]
                term = lax.dot_general(parts[i], block, NT, preferred_element_type=F32)
                if i == 0:
                    out_ref[rows, :] = term
                else:
                    out_ref[rows, :] += term
        whole = jnp.concatenate(parts, axis=1)
        out_ref[2 * RANK :, :] = jnp.zeros((EXTRA, depth), F32)
        out_ref[2 * RANK :, 0:LANES] = pack(self_gram(whole))

    return pl.pallas_call(
        kernel,
        out_shape=jax.ShapeDtypeStruct((2 * RANK + EXTRA, depth), F32),
        in_specs=[
            pl.BlockSpec(memory_space=pltpu.VMEM),
            pl.BlockSpec(memory_space=pltpu.VMEM),
            pl.BlockSpec(memory_space=pltpu.VMEM),
        ],
        out_specs=pl.BlockSpec(memory_space=pltpu.VMEM),
        compiler_params=pltpu.CompilerParams(vmem_limit_bytes=MID_BYTES),
        name="partial_sketch",
    )(h, a, mate)


def product_step(hours, keep, mine, other, a, mate, l_inv=None):
    half, depth, width = mate.shape
    narrow = l_inv is not None
    operands = (mine, other, a, mate) + ((l_inv,) if narrow else ())

    def kernel(mine_ref, other_ref, a_ref, mate_ref, *rest_refs):
        out_ref = rest_refs[-1]
        gram = mine_ref[2 * RANK :, 0:LANES] + other_ref[2 * RANK :, 0:LANES]
        v_inv = inverse_factor(gram, True) * float(hours) ** 0.5
        if narrow:
            v_inv = jnp.dot(rest_refs[0][...], v_inv, precision=HIGH, preferred_element_type=F32)
        own = mine_ref[0:RANK, :] + other_ref[RANK : 2 * RANK, :]
        own = jnp.dot(v_inv, own, precision=HIGH, preferred_element_type=F32)
        far = mine_ref[RANK : 2 * RANK, :] + other_ref[0:RANK, :]
        far = jnp.dot(v_inv, far, precision=HIGH, preferred_element_type=F32)
        gram = pack(self_gram(own, HIGH) + self_gram(far, HIGH))
        left = split_bf16(own)
        right = split_bf16(far)
        kept = own.astype(BF16)
        for i in range(half):
            both = jnp.dot(left, a_ref[lax.axis_index("c") * half + i, 0:depth, :], preferred_element_type=F32)
            both = both + jnp.dot(right, mate_ref[i], preferred_element_type=F32)
            part = both[0:RANK] + both[RANK : 2 * RANK]
            if not narrow:
                store_part(out_ref, i, part, gram)
                continue
            for side in range(2):
                k = 2 * i + side
                out_ref[k, 0:RANK, :] = part[:, side * LANES : (side + 1) * LANES].astype(BF16)
                out_ref[k, RANK:NARROW, :] = split_bf16(gram)
                for j in range(depth // LANES if keep else 0):
                    rows = slice(NARROW + j * RANK, NARROW + (j + 1) * RANK)
                    out_ref[k, rows, :] = kept[:, j * LANES : (j + 1) * LANES]

    out_shape = jax.ShapeDtypeStruct((2 * half, ROWS, LANES), F32)
    if narrow:
        height = NARROW + (RANK * depth // LANES if keep else 0)
        out_shape = jax.ShapeDtypeStruct((2 * half, height, LANES), BF16)
    return pl.pallas_call(
        kernel,
        out_shape=out_shape,
        in_specs=[pl.BlockSpec(memory_space=pltpu.VMEM)] * len(operands),
        out_specs=pl.BlockSpec(memory_space=pltpu.VMEM),
        compiler_params=pltpu.CompilerParams(vmem_limit_bytes=MID_BYTES),
        name="hour_products",
    )(*operands)


def sum_parts(ref):
    rows = ROWS if ref.dtype == F32 else NARROW
    total = ref[0, 0:rows, :].astype(F32)
    for k in range(1, ref.shape[0]):
        total = total + ref[k, 0:rows, :].astype(F32)
    if rows == ROWS:
        return total
    return jnp.concatenate([total[0:RANK], total[RANK:ROWS] + total[ROWS:NARROW]], axis=0)


def sum_step(parts, copies):
    narrow = parts.dtype == BF16

    def kernel(in_ref, out_ref):
        total = sum_parts(in_ref)
        if narrow:
            total = jnp.concatenate([total[0:RANK].astype(BF16), split_bf16(total[RANK:ROWS])], axis=0)
        for k in range(copies):
            out_ref[k] = total

    return pl.pallas_call(
        kernel,
        out_shape=jax.ShapeDtypeStruct(
            (copies, NARROW if narrow else ROWS, LANES), BF16 if narrow else F32
        ),
        in_specs=[pl.BlockSpec(memory_space=pltpu.VMEM)],
        out_specs=pl.BlockSpec(memory_space=pltpu.VMEM),
        compiler_params=pltpu.CompilerParams(vmem_limit_bytes=SMALL_BYTES),
        name="sum_parts",
    )(parts)


def hour_step(parts, copies, points, last, l_prev=None):
    operands = (parts,) if l_prev is None else (parts, l_prev)

    def kernel(in_ref, *refs):
        outs = refs[len(operands) - 1 :]
        total = sum_parts(in_ref)
        l_inv = inverse_factor(total[RANK:ROWS], False) * float(points) ** 0.5
        hours = jnp.dot(l_inv, total[0:RANK], precision=HIGH, preferred_element_type=F32)
        if last:
            outs[1][...] = l_inv
        if l_prev is not None:
            l_inv = jnp.dot(l_inv, refs[0][...], precision=HIGH, preferred_element_type=F32)
        if not last:
            outs[1][...] = l_inv
        hours = lax.dot_general(l_inv, hours, TN, precision=HIGH, preferred_element_type=F32)
        if last:
            gram = packed_gram(hours)
            for k in range(copies):
                outs[0][k] = gram
            outs[2][...] = hours
        else:
            rounded = hours.astype(BF16)
            for k in range(copies):
                outs[0][k] = rounded

    out_shape = [
        jax.ShapeDtypeStruct((copies, EXTRA, LANES), F32) if last else jax.ShapeDtypeStruct((copies, RANK, LANES), BF16),
        jax.ShapeDtypeStruct((RANK, RANK), F32),
    ]
    if last:
        out_shape.append(jax.ShapeDtypeStruct((RANK, LANES), F32))
    return pl.pallas_call(
        kernel,
        out_shape=out_shape,
        in_specs=[pl.BlockSpec(memory_space=pltpu.VMEM)] * len(operands),
        out_specs=[pl.BlockSpec(memory_space=pltpu.VMEM)] * len(out_shape),
        compiler_params=pltpu.CompilerParams(vmem_limit_bytes=SMALL_BYTES),
        name="row_factor",
    )(*operands)


def column_step(grams, mine, other, hours):
    def kernel(gram_ref, mine_ref, other_ref, out_ref):
        total = gram_ref[0]
        for k in range(1, grams.shape[0]):
            total = total + gram_ref[k]
        v_inv = inverse_factor(total, True) * float(hours) ** 0.5
        first = lax.axis_index("c") == 0
        low = jnp.where(first, mine_ref[...], other_ref[...])
        high = jnp.where(first, other_ref[...], mine_ref[...])
        block = jnp.concatenate([low, high], axis=1)
        out_ref[...] = jnp.dot(v_inv, block, precision=HIGH, preferred_element_type=F32)

    return pl.pallas_call(
        kernel,
        out_shape=jax.ShapeDtypeStruct((RANK, 2 * LANES), F32),
        in_specs=[pl.BlockSpec(memory_space=pltpu.VMEM)] * 3,
        out_specs=pl.BlockSpec(memory_space=pltpu.VMEM),
        compiler_params=pltpu.CompilerParams(vmem_limit_bytes=SMALL_BYTES),
        name="column_factor",
    )(grams, mine, other)


def row_step(l_inv, parts):
    blocks, height, _ = parts.shape
    pieces = (height - NARROW) // RANK
    depth = pieces * LANES
    group = 4

    def kernel(l_ref, s_ref, out_ref):
        left = split_bf16(l_ref[...])
        for k in range(group):
            rows = [s_ref[k, NARROW + j * RANK : NARROW + (j + 1) * RANK, :] for j in range(pieces)]
            out = jnp.dot(left, jnp.concatenate(rows, axis=1), preferred_element_type=F32)
            out_ref[:, k * depth : (k + 1) * depth] = out[0:RANK] + out[RANK : 2 * RANK]

    return pl.pallas_call(
        kernel,
        grid=(blocks // group,),
        out_shape=jax.ShapeDtypeStruct((RANK, blocks * depth), F32),
        in_specs=[
            pl.BlockSpec((RANK, RANK), lambda i: (0, 0)),
            pl.BlockSpec((group, height, LANES), lambda i: (i, 0, 0)),
        ],
        out_specs=pl.BlockSpec((RANK, group * depth), lambda i: (0, i)),
        cost_estimate=pl.CostEstimate(
            flops=4 * RANK * RANK * blocks * depth, bytes_accessed=6 * RANK * blocks * depth, transcendentals=0
        ),
        compiler_params=pltpu.CompilerParams(vmem_limit_bytes=SMALL_BYTES),
        name="row_basis",
    )(l_inv, parts)


def ring(size, shift):
    return [(i, (i + shift) % size) for i in range(size)]


def solution(mesh):
    grid_size, tm_size = mesh.devices.shape
    fine = Mesh(mesh.devices.reshape(grid_size // 2, 2, tm_size), ("z", "c", "t"))

    def shards(anomaly, start_basis):
        points = anomaly.shape[0] * grid_size
        hours = anomaly.shape[1] * tm_size
        depth = anomaly.shape[0] // tm_size
        a = append_basis(anomaly.reshape(tm_size, depth, anomaly.shape[1]), start_basis)
        a = lax.all_to_all(a, "t", 0, 0)
        swap = ring(2, 1)
        out, send = first_step(a)
        mate = lax.ppermute(send, "c", swap)
        part = lax.all_to_all(out, ("c", "t"), 0, 0)
        for step in range(ITERS):
            last = step == ITERS - 1
            l_prev = l_inv if step > 1 else None
            if step:
                sketch = sketch_step(h, a, mate)
                other = lax.ppermute(sketch, "c", swap)
                out = product_step(hours, last, sketch, other, a, mate, l_prev)
                part = lax.all_to_all(out, "t", 0, 0)
                if last:
                    rows = part
            part = sum_step(part, grid_size // 2)
            part = lax.all_to_all(part, "z", 0, 0)
            h, l_inv, *whole = hour_step(part, (2 if last else 1) * tm_size, points, last, l_prev)
            h = lax.all_to_all(h, ("c", "t") if last else "t", 0, 0)
        home = [(i, i % 2 * tm_size + i // 2) for i in range(2 * tm_size)]
        mine = lax.ppermute(whole[0], ("c", "t"), home)
        other = lax.ppermute(mine, "c", swap)
        return row_step(l_inv, rows), column_step(h, mine, other, hours)

    return jax.shard_map(
        shards,
        mesh=fine,
        in_specs=(P(("z", "c"), "t"), P(None, "t")),
        out_specs=(P(None, ("z", "c")), P(None, "t")),
        check_vma=False,
    )
```

```python
import jax
import jax.numpy as jnp
from jax import lax
from jax.experimental import pallas as pl
from jax.experimental.pallas import tpu as pltpu
from jax.sharding import Mesh, PartitionSpec as P

ITERS = 6
RANK = 32
LANES = 128
EXTRA = RANK * RANK // LANES
ROWS = RANK + EXTRA
NARROW = RANK + 2 * EXTRA
SMALL_BYTES = 4 * 1024 * 1024
MID_BYTES = 20 * 1024 * 1024
F32 = jnp.float32
BF16 = jnp.bfloat16
HIGH = lax.Precision.HIGHEST
NT = (((1,), (1,)), ((), ()))
TN = (((0,), (0,)), ((), ()))


def split_f32(value):
    high = value.astype(BF16)
    return high, value - high.astype(F32)


def split_bf16(value):
    high, low = split_f32(value)
    return jnp.concatenate([high, low.astype(BF16)], axis=0)


def pack(gram):
    return jnp.concatenate([gram[b * EXTRA : (b + 1) * EXTRA] for b in range(RANK // EXTRA)], axis=1)


def self_gram(block, precision=None):
    return lax.dot_general(block, block, NT, precision=precision, preferred_element_type=F32)


def packed_gram(block):
    return pack(self_gram(block, HIGH))


def inverse_factor(packed, upper):
    parts = RANK // EXTRA
    shape = (EXTRA, LANES)
    lane = lax.broadcasted_iota(jnp.int32, shape, 1)
    sub = lax.broadcasted_iota(jnp.int32, shape, 0)
    work = []
    for b in range(parts):
        shift = (RANK - b * RANK) % LANES
        gram = pltpu.roll(packed, shift, 1) if shift else packed
        gram = jnp.where(lane < 2 * RANK, gram, 0.0)
        work.append(jnp.where(lane < RANK, (lane == sub + b * EXTRA).astype(F32), gram))
    scale = []
    places = range(EXTRA - 1, -1, -1) if upper else range(EXTRA)
    for block in range(parts - 1, -1, -1) if upper else range(parts):
        beyond = range(block) if upper else range(block + 1, parts)
        cols = {
            b: [jnp.broadcast_to(work[b][:, c : c + 1], shape) for c in [RANK + block * EXTRA + r for r in places]]
            for b in (block, *beyond)
        }
        rows = [jnp.broadcast_to(work[block][r : r + 1, :], shape) for r in places]
        pivots = [[jnp.broadcast_to(col[r : r + 1, :], shape) for col in cols[block]] for r in places]
        scaled = []
        final = work[block]
        diagonal = pivots[0][0]
        for i, r in enumerate(places):
            inverse = 1.0 / pivots[i][i]
            for j in range(i + 1, EXTRA):
                factor = pivots[i][j] * inverse
                for k in range(j, EXTRA):
                    pivots[j][k] = pivots[j][k] - factor * pivots[i][k]
                rows[j] = rows[j] - factor * rows[i]
                for b in beyond:
                    cols[b][j] = cols[b][j] - factor * cols[b][i]
            scaled.append(rows[i] * inverse)
            final = jnp.where(sub == r, rows[i], final)
            diagonal = jnp.where(sub == r, pivots[i][i], diagonal)
        work[block] = final
        scale.append((block, diagonal))
        for b in beyond:
            for i in range(EXTRA):
                work[b] = work[b] - cols[b][i] * scaled[i]
    rows = [work[b] / jnp.sqrt(diagonal) for b, diagonal in sorted(scale, key=lambda item: item[0])]
    return jnp.concatenate(rows, axis=0)[:, :RANK]


def append_basis(a, basis):
    blocks, depth, width = a.shape

    def kernel(a_ref, basis_ref, out_ref, sems):
        def load(t):
            return pltpu.make_async_copy(a_ref.at[t], out_ref.at[t, 0:depth, :], sems.at[t])

        for t in range(blocks):
            load(t).start()
        for t in range(blocks):
            out_ref[t, depth : depth + RANK, :] = basis_ref[...]
        for t in range(blocks):
            load(t).wait()

    return pl.pallas_call(
        kernel,
        out_shape=jax.ShapeDtypeStruct((blocks, depth + RANK, width), BF16),
        in_specs=[pl.BlockSpec(memory_space=pl.ANY), pl.BlockSpec(memory_space=pltpu.VMEM)],
        out_specs=pl.BlockSpec(memory_space=pltpu.VMEM),
        scratch_shapes=[pltpu.SemaphoreType.DMA((blocks,))],
        compiler_params=pltpu.CompilerParams(vmem_limit_bytes=MID_BYTES),
        name="append_basis",
    )(a, basis)


def first_step(a):
    blocks, depth, width = a.shape
    depth -= RANK
    half = blocks // 2

    def kernel(a_ref, out_ref, send_ref, acc, send_sems):
        def send(i):
            t = (1 - lax.axis_index("c")) * half + i
            return pltpu.make_async_copy(a_ref.at[t, 0:depth, :], send_ref.at[i], send_sems.at[i])

        for i in range(half):
            send(i).start()
        for t in range(blocks):
            basis = a_ref[t, depth : depth + RANK, :]
            term = lax.dot_general(basis, a_ref[t, 0:depth, :], NT, preferred_element_type=F32)
            if t == 0:
                acc[...] = term
            else:
                acc[...] += term
        sketch = acc[...]
        gram = packed_gram(sketch)
        left = split_bf16(sketch)
        for t in range(blocks):
            both = jnp.dot(left, a_ref[t, 0:depth, :], preferred_element_type=F32)
            store_part(out_ref, t, both[0:RANK] + both[RANK : 2 * RANK], gram)
        for i in range(half):
            send(i).wait()

    return pl.pallas_call(
        kernel,
        out_shape=[
            jax.ShapeDtypeStruct((2 * blocks, ROWS, LANES), F32),
            jax.ShapeDtypeStruct((half, depth, width), BF16),
        ],
        in_specs=[pl.BlockSpec(memory_space=pltpu.VMEM)],
        out_specs=[pl.BlockSpec(memory_space=pltpu.VMEM), pl.BlockSpec(memory_space=pl.ANY)],
        scratch_shapes=[pltpu.VMEM((RANK, depth), F32), pltpu.SemaphoreType.DMA((half,))],
        compiler_params=pltpu.CompilerParams(vmem_limit_bytes=MID_BYTES),
        name="first_products",
    )(a)


def store_part(out_ref, block, part, gram):
    for side in range(2):
        out_ref[2 * block + side, 0:RANK, :] = part[:, side * LANES : (side + 1) * LANES]
        out_ref[2 * block + side, RANK:ROWS, :] = gram


def sketch_step(h, a, mate):
    half, depth, width = mate.shape

    def kernel(h_ref, a_ref, mate_ref, out_ref):
        whole = jnp.concatenate([h_ref[k] for k in range(2 * half)], axis=1)
        base = lax.axis_index("c") * half
        span = depth // 4
        for start in range(0, depth, span):
            rows = slice(start, start + span)
            own = jnp.concatenate([a_ref[base + i, rows, :] for i in range(half)], axis=1)
            far = jnp.concatenate([mate_ref[i, rows, :] for i in range(half)], axis=1)
            out_ref[0:RANK, rows] = lax.dot_general(whole, own, NT, preferred_element_type=F32)
            out_ref[RANK : 2 * RANK, rows] = lax.dot_general(far, whole, NT, preferred_element_type=F32).T
        out_ref[2 * RANK :, :] = jnp.zeros((EXTRA, depth), F32)
        out_ref[2 * RANK :, 0:LANES] = pack(self_gram(whole))

    return pl.pallas_call(
        kernel,
        out_shape=jax.ShapeDtypeStruct((2 * RANK + EXTRA, depth), F32),
        in_specs=[
            pl.BlockSpec(memory_space=pltpu.VMEM),
            pl.BlockSpec(memory_space=pltpu.VMEM),
            pl.BlockSpec(memory_space=pltpu.VMEM),
        ],
        out_specs=pl.BlockSpec(memory_space=pltpu.VMEM),
        compiler_params=pltpu.CompilerParams(vmem_limit_bytes=MID_BYTES),
        name="partial_sketch",
    )(h, a, mate)


def product_step(hours, keep, mine, other, a, mate, l_inv=None):
    half, depth, width = mate.shape
    narrow = l_inv is not None
    operands = (mine, other, a, mate) + ((l_inv,) if narrow else ())

    def kernel(mine_ref, other_ref, a_ref, mate_ref, *rest_refs):
        out_ref = rest_refs[-1]
        gram = mine_ref[2 * RANK :, 0:LANES] + other_ref[2 * RANK :, 0:LANES]
        v_inv = inverse_factor(gram, True) * float(hours) ** 0.5
        if narrow:
            v_inv = jnp.dot(rest_refs[0][...], v_inv, precision=HIGH, preferred_element_type=F32)
        own = mine_ref[0:RANK, :] + other_ref[RANK : 2 * RANK, :]
        own = jnp.dot(v_inv, own, precision=HIGH, preferred_element_type=F32)
        far = mine_ref[RANK : 2 * RANK, :] + other_ref[0:RANK, :]
        far = jnp.dot(v_inv, far, precision=HIGH, preferred_element_type=F32)
        gram = pack(self_gram(own, HIGH) + self_gram(far, HIGH))
        left = split_bf16(own)
        right = split_bf16(far)
        kept = own.astype(BF16)
        for i in range(half):
            both = jnp.dot(left, a_ref[lax.axis_index("c") * half + i, 0:depth, :], preferred_element_type=F32)
            both = both + jnp.dot(right, mate_ref[i], preferred_element_type=F32)
            part = both[0:RANK] + both[RANK : 2 * RANK]
            if not narrow:
                store_part(out_ref, i, part, gram)
                continue
            for side in range(2):
                k = 2 * i + side
                out_ref[k, 0:RANK, :] = part[:, side * LANES : (side + 1) * LANES].astype(BF16)
                out_ref[k, RANK:NARROW, :] = split_bf16(gram)
                for j in range(depth // LANES if keep else 0):
                    rows = slice(NARROW + j * RANK, NARROW + (j + 1) * RANK)
                    out_ref[k, rows, :] = kept[:, j * LANES : (j + 1) * LANES]

    out_shape = jax.ShapeDtypeStruct((2 * half, ROWS, LANES), F32)
    if narrow:
        height = NARROW + (RANK * depth // LANES if keep else 0)
        out_shape = jax.ShapeDtypeStruct((2 * half, height, LANES), BF16)
    return pl.pallas_call(
        kernel,
        out_shape=out_shape,
        in_specs=[pl.BlockSpec(memory_space=pltpu.VMEM)] * len(operands),
        out_specs=pl.BlockSpec(memory_space=pltpu.VMEM),
        compiler_params=pltpu.CompilerParams(vmem_limit_bytes=MID_BYTES),
        name="hour_products",
    )(*operands)


def sum_parts(ref):
    rows = ROWS if ref.dtype == F32 else NARROW
    total = ref[0, 0:rows, :].astype(F32)
    for k in range(1, ref.shape[0]):
        total = total + ref[k, 0:rows, :].astype(F32)
    if rows == ROWS:
        return total
    return jnp.concatenate([total[0:RANK], total[RANK:ROWS] + total[ROWS:NARROW]], axis=0)


def sum_step(parts, copies):
    narrow = parts.dtype == BF16

    def kernel(in_ref, out_ref):
        total = sum_parts(in_ref)
        if narrow:
            total = jnp.concatenate([total[0:RANK].astype(BF16), split_bf16(total[RANK:ROWS])], axis=0)
        for k in range(copies):
            out_ref[k] = total

    return pl.pallas_call(
        kernel,
        out_shape=jax.ShapeDtypeStruct(
            (copies, NARROW if narrow else ROWS, LANES), BF16 if narrow else F32
        ),
        in_specs=[pl.BlockSpec(memory_space=pltpu.VMEM)],
        out_specs=pl.BlockSpec(memory_space=pltpu.VMEM),
        compiler_params=pltpu.CompilerParams(vmem_limit_bytes=SMALL_BYTES),
        name="sum_parts",
    )(parts)


def hour_step(parts, copies, points, last, l_prev=None):
    operands = (parts,) if l_prev is None else (parts, l_prev)

    def kernel(in_ref, *refs):
        outs = refs[len(operands) - 1 :]
        total = sum_parts(in_ref)
        l_inv = inverse_factor(total[RANK:ROWS], False) * float(points) ** 0.5
        hours = jnp.dot(l_inv, total[0:RANK], precision=HIGH, preferred_element_type=F32)
        if last:
            outs[1][...] = l_inv
        if l_prev is not None:
            l_inv = jnp.dot(l_inv, refs[0][...], precision=HIGH, preferred_element_type=F32)
        if not last:
            outs[1][...] = l_inv
        hours = lax.dot_general(l_inv, hours, TN, precision=HIGH, preferred_element_type=F32)
        if last:
            gram = packed_gram(hours)
            for k in range(copies):
                outs[0][k] = gram
            outs[2][...] = hours
        else:
            rounded = hours.astype(BF16)
            for k in range(copies):
                outs[0][k] = rounded

    out_shape = [
        jax.ShapeDtypeStruct((copies, EXTRA, LANES), F32) if last else jax.ShapeDtypeStruct((copies, RANK, LANES), BF16),
        jax.ShapeDtypeStruct((RANK, RANK), F32),
    ]
    if last:
        out_shape.append(jax.ShapeDtypeStruct((RANK, LANES), F32))
    return pl.pallas_call(
        kernel,
        out_shape=out_shape,
        in_specs=[pl.BlockSpec(memory_space=pltpu.VMEM)] * len(operands),
        out_specs=[pl.BlockSpec(memory_space=pltpu.VMEM)] * len(out_shape),
        compiler_params=pltpu.CompilerParams(vmem_limit_bytes=SMALL_BYTES),
        name="row_factor",
    )(*operands)


def column_step(grams, mine, other, hours):
    def kernel(gram_ref, mine_ref, other_ref, out_ref):
        total = gram_ref[0]
        for k in range(1, grams.shape[0]):
            total = total + gram_ref[k]
        v_inv = inverse_factor(total, True) * float(hours) ** 0.5
        first = lax.axis_index("c") == 0
        low = jnp.where(first, mine_ref[...], other_ref[...])
        high = jnp.where(first, other_ref[...], mine_ref[...])
        block = jnp.concatenate([low, high], axis=1)
        out_ref[...] = jnp.dot(v_inv, block, precision=HIGH, preferred_element_type=F32)

    return pl.pallas_call(
        kernel,
        out_shape=jax.ShapeDtypeStruct((RANK, 2 * LANES), F32),
        in_specs=[pl.BlockSpec(memory_space=pltpu.VMEM)] * 3,
        out_specs=pl.BlockSpec(memory_space=pltpu.VMEM),
        compiler_params=pltpu.CompilerParams(vmem_limit_bytes=SMALL_BYTES),
        name="column_factor",
    )(grams, mine, other)


def row_step(l_inv, parts):
    blocks, height, _ = parts.shape
    pieces = (height - NARROW) // RANK
    depth = pieces * LANES
    group = 4

    def kernel(l_ref, s_ref, out_ref):
        left = split_bf16(l_ref[...])
        for k in range(group):
            rows = [s_ref[k, NARROW + j * RANK : NARROW + (j + 1) * RANK, :] for j in range(pieces)]
            out = jnp.dot(left, jnp.concatenate(rows, axis=1), preferred_element_type=F32)
            out_ref[:, k * depth : (k + 1) * depth] = out[0:RANK] + out[RANK : 2 * RANK]

    return pl.pallas_call(
        kernel,
        grid=(blocks // group,),
        out_shape=jax.ShapeDtypeStruct((RANK, blocks * depth), F32),
        in_specs=[
            pl.BlockSpec((RANK, RANK), lambda i: (0, 0)),
            pl.BlockSpec((group, height, LANES), lambda i: (i, 0, 0)),
        ],
        out_specs=pl.BlockSpec((RANK, group * depth), lambda i: (0, i)),
        cost_estimate=pl.CostEstimate(
            flops=4 * RANK * RANK * blocks * depth, bytes_accessed=6 * RANK * blocks * depth, transcendentals=0
        ),
        compiler_params=pltpu.CompilerParams(vmem_limit_bytes=SMALL_BYTES),
        name="row_basis",
    )(l_inv, parts)


def ring(size, shift):
    return [(i, (i + shift) % size) for i in range(size)]


def solution(mesh):
    grid_size, tm_size = mesh.devices.shape
    fine = Mesh(mesh.devices.reshape(grid_size // 2, 2, tm_size), ("z", "c", "t"))

    def shards(anomaly, start_basis):
        points = anomaly.shape[0] * grid_size
        hours = anomaly.shape[1] * tm_size
        depth = anomaly.shape[0] // tm_size
        a = append_basis(anomaly.reshape(tm_size, depth, anomaly.shape[1]), start_basis)
        a = lax.all_to_all(a, "t", 0, 0)
        swap = ring(2, 1)
        out, send = first_step(a)
        mate = lax.ppermute(send, "c", swap)
        part = lax.all_to_all(out, ("c", "t"), 0, 0)
        for step in range(ITERS):
            last = step == ITERS - 1
            l_prev = l_inv if step > 1 else None
            if step:
                sketch = sketch_step(h, a, mate)
                other = lax.ppermute(sketch, "c", swap)
                out = product_step(hours, last, sketch, other, a, mate, l_prev)
                part = lax.all_to_all(out, "t", 0, 0)
                if last:
                    rows = part
            part = sum_step(part, grid_size // 2)
            part = lax.all_to_all(part, "z", 0, 0)
            h, l_inv, *whole = hour_step(part, (2 if last else 1) * tm_size, points, last, l_prev)
            h = lax.all_to_all(h, ("c", "t") if last else "t", 0, 0)
        home = [(i, i % 2 * tm_size + i // 2) for i in range(2 * tm_size)]
        mine = lax.ppermute(whole[0], ("c", "t"), home)
        other = lax.ppermute(mine, "c", swap)
        return row_step(l_inv, rows), column_step(h, mine, other, hours)

    return jax.shard_map(
        shards,
        mesh=fine,
        in_specs=(P(("z", "c"), "t"), P(None, "t")),
        out_specs=(P(None, ("z", "c")), P(None, "t")),
        check_vma=False,
    )
```
